512 devices in a mesh: blk: 128 (over x, z, y_hi), grp: 4 (over y_lo, core).
Axes of the slice: x: 4, y: 4 (y_hi: 2, y_lo: 2; y = y_hi * 2 + y_lo), z: 16, core: 2. Of those that a mesh axis runs over, the one named last changes fastest.
Arguments:
- values: bfloat16 [128, 4, 6, 64, 4096], P('blk', 'grp'), may hold values from -96 to 96
- counts: int32 [128, 4], P('blk', 'grp'), may hold values from 1 to 6, as said below
- row_block: int32 [128, 4, 6], P('blk', 'grp'), may hold values from 0 to 1
- col_block: int32 [128, 4, 6], P('blk', 'grp'), may hold values from 0 to 127
- depth_block: int32 [128, 4, 6], P('blk', 'grp'), may hold values from 0 to 3
- factor_b: bfloat16 [8192, 256], P('blk')
- factor_c: bfloat16 [1024, 256], P('grp')
- fetch_list: int32 [128, 4, 64], P('blk', 'grp'), may hold values from 0 to 255, as said below
Outputs:
- a_new: bfloat16 [16384, 256], P(('blk', 'grp'))
- fetched: bfloat16 [128, 4, 64, 4096], P('blk', 'grp')
The draws below stay inside these ranges and needn't reach their ends.
Inputs may be any that keep to these rules, and one draw needn't show every extreme that they name: `counts`: each device has 1 to 6 live slots; some device has exactly 6; slots beyond the live ones hold values that must not count. `fetch_list`: entry f of a device names unit f mod 2 of blk index f div 2, in the device's own index of grp; the 64 entries of one device name 64 distinct indices of blk.
All inputs are finite; a program needn't handle non-finite values.
Results may differ from the reference program's by a relative error of at most 0.00185.
Values may be sent and summed in bfloat16 or wider, within the bound.
A program may use at most 64 MiB of HBM per device.

```python
import jax
import jax.numpy as jnp
from jax import lax

R = 256
EDGE = 64
NB = 6
IBD = 2
JBD = 1
KB = 4
UNIT = 16
SLOTS = 64
NI = 16384
NJ = 8192
NK = 1024
N_BLK = 128
N_GRP = 4


def shared_factor(key, rows, shared):
    key_noise = jax.random.fold_in(key, 21)
    key_rows = jax.random.fold_in(key, 22)
    key_load = jax.random.fold_in(key, 23)
    noise = jax.random.normal(key_noise, (rows, R), jnp.float32)
    common = jax.random.normal(key_rows, (rows, 1), jnp.float32)
    loading = jax.random.normal(key_load, (1, R), jnp.float32)
    return ((noise + shared * common * loading) / jnp.sqrt(jnp.float32(rows))).astype(jnp.bfloat16)


def draw_factor_b(key, part):
    key = jax.random.fold_in(key, 3)
    return shared_factor(key, NJ, 0.6)


def draw_factor_c(key, part):
    key = jax.random.fold_in(key, 4)
    return shared_factor(key, NK, 0.5)


def draw_counts(key, part):
    key = jax.random.fold_in(key, 1)
    drawn = jax.random.randint(key, (N_BLK * N_GRP,), 1, NB + 1, dtype=jnp.int32)
    chosen = jax.random.randint(jax.random.fold_in(key, 11), (), 0, N_BLK * N_GRP, dtype=jnp.int32)
    filled = jnp.where(jnp.arange(N_BLK * N_GRP, dtype=jnp.int32) == chosen, NB, drawn)
    return filled.reshape(N_BLK, N_GRP).astype(jnp.int32)


def draw_fetch_list(key, part):
    key = jax.random.fold_in(key, 2)
    keys = jax.random.split(key, N_BLK * N_GRP)
    peers = jax.vmap(lambda single: jax.random.permutation(single, N_BLK)[:SLOTS])(keys)
    within = jax.random.randint(jax.random.fold_in(key, 12), (N_BLK * N_GRP, SLOTS), 0, IBD, dtype=jnp.int32)
    return (peers.astype(jnp.int32) * IBD + within).reshape(N_BLK, N_GRP, SLOTS).astype(jnp.int32)


def touch_ends(values, key, smallest, top_value):
    longest = values.shape.index(max(values.shape))
    spots = []
    for shift in (0, 1):
        where = [jax.random.randint(jax.random.fold_in(key, axis), (), 0, length) for axis, length in enumerate(values.shape)]
        where[longest] = (where[longest] + shift) % values.shape[longest]
        spots.append(tuple(where))
    return values.at[spots[0]].set(smallest).at[spots[1]].set(top_value)


def level_of(rng, shape, cuts, low, largest):
    def one(dim, parts):
        heights = jax.random.uniform(jax.random.fold_in(jax.random.fold_in(rng, 6), dim), (parts,), jnp.float32, low / len(cuts), largest / len(cuts))
        return jnp.repeat(jnp.exp(heights), shape[dim] // parts).reshape((-1,) + (1,) * (len(shape) - dim - 1))

    gain = one(*cuts[0])
    for cut in cuts[1:]:
        gain = gain * one(*cut)
    return gain


def bell_draw(rng, extent, width, most, cuts=(), kind=jnp.bfloat16):
    array = width * jax.random.normal(rng, extent, jnp.float32)
    if cuts:
        array = array * level_of(rng, extent, cuts, -0.22, 0.18)
    return jnp.clip(array, -most, most).astype(kind)


def setup_inputs(seed: int = 0) -> dict:
    streams_of = jax.random.split(jax.random.key(seed), 9)
    return {
        "values": bell_draw(streams_of[0], (N_BLK, N_GRP, NB, EDGE, EDGE * EDGE), 16.0, 96.0, ((0, 128), (1, 4))),
        "counts": draw_counts(jax.random.fold_in(streams_of[8], 71), 0),
        "row_block": touch_ends(jax.random.randint(streams_of[2], (N_BLK, N_GRP, NB), 0, IBD), jax.random.fold_in(streams_of[2], 1), 0, IBD - 1).astype(jnp.int32),
        "col_block": touch_ends(jax.random.randint(streams_of[3], (N_BLK, N_GRP, NB), 0, JBD * N_BLK), jax.random.fold_in(streams_of[3], 1), 0, (JBD * N_BLK) - 1).astype(jnp.int32),
        "depth_block": touch_ends(jax.random.randint(streams_of[4], (N_BLK, N_GRP, NB), 0, KB), jax.random.fold_in(streams_of[4], 1), 0, KB - 1).astype(jnp.int32),
        "factor_b": draw_factor_b(jax.random.fold_in(streams_of[8], 71), 0),
        "factor_c": draw_factor_c(jax.random.fold_in(streams_of[8], 71), 0),
        "fetch_list": draw_fetch_list(jax.random.fold_in(streams_of[8], 71), 0),
    }


def reference(values, counts, row_block, col_block, depth_block, factor_b, factor_c, fetch_list):
    total = N_BLK * N_GRP * NB
    flat = values.reshape(total, EDGE, EDGE * EDGE)
    blk_index = jnp.arange(N_BLK, dtype=jnp.int32)[:, None, None]
    grp_index = jnp.arange(N_GRP, dtype=jnp.int32)[None, :, None]
    slot_index = jnp.arange(NB, dtype=jnp.int32)[None, None, :]
    alive = (slot_index < counts[:, :, None]).astype(jnp.float32)
    col_start = (col_block * EDGE).astype(jnp.int32)
    depth_start = ((grp_index * KB + depth_block) * EDGE).astype(jnp.int32)
    segment = (blk_index * IBD + row_block).astype(jnp.int32)

    def one_block(items):
        cube, cstart, dstart, live = items
        depth_rows = lax.dynamic_slice_in_dim(factor_c, dstart, EDGE, 0)
        product = jnp.dot(cube.reshape(EDGE * EDGE, EDGE).astype(jnp.float32), depth_rows.astype(jnp.float32), preferred_element_type=jnp.float32)
        product = product.reshape(EDGE, EDGE, R)
        column_rows = lax.dynamic_slice_in_dim(factor_b, cstart, EDGE, 0).astype(jnp.float32)
        term = jnp.sum(product * column_rows[None, :, :], axis=1)
        return term * live
    terms = lax.map(one_block, (flat, col_start.reshape(-1), jnp.broadcast_to(depth_start, (N_BLK, N_GRP, NB)).reshape(-1), alive.reshape(-1)))
    mttkrp = jax.ops.segment_sum(terms, jnp.broadcast_to(segment, (N_BLK, N_GRP, NB)).reshape(-1), num_segments=N_BLK * IBD)
    mttkrp = mttkrp.reshape(NI, R)
    gram_b = jnp.einsum('jr,js->rs', factor_b.astype(jnp.float32), factor_b.astype(jnp.float32), preferred_element_type=jnp.float32)
    gram_c = jnp.einsum('kr,ks->rs', factor_c.astype(jnp.float32), factor_c.astype(jnp.float32), preferred_element_type=jnp.float32)
    system = gram_b * gram_c
    lower = jnp.linalg.cholesky(system)
    solved = jax.scipy.linalg.cho_solve((lower, True), mttkrp.T).T
    a_new = solved.astype(jnp.bfloat16)
    units = a_new.reshape(N_BLK * N_GRP * IBD, UNIT * R)
    owner = (fetch_list // IBD).astype(jnp.int32)
    within = (fetch_list % IBD).astype(jnp.int32)
    unit_index = ((owner * N_GRP + grp_index) * IBD + within).astype(jnp.int32)
    fetched = units[unit_index]
    return (a_new, fetched)
```

```python
import functools

import jax
import jax.numpy as jnp
from jax import lax
from jax.experimental import pallas as pl
from jax.experimental.pallas import tpu as pltpu
from jax.sharding import PartitionSpec as P

MESH = pl.DeviceIdType.MESH
NX, NZ, NY, NC = 4, 16, 4, 2
YH = 2
R = 256
EDGE = 64
NB = 6
PIECE = 16
ROWS = 32
SLOTS = 64
F32 = jnp.float32
BF16 = jnp.bfloat16


def place():
    b, g = lax.axis_index("blk"), lax.axis_index("grp")
    x, z, yh = b // (NZ * YH), (b // YH) % NZ, b % YH
    return x, z, yh * 2 + g // NC, g % NC


def device(x, z, y, c):
    return ((x * NZ + z) * YH + y // 2, (y % 2) * NC + c)


def greet(others):
    barrier = pltpu.get_barrier_semaphore()
    for other in others:
        pl.semaphore_signal(barrier, inc=1, device_id=other, device_id_type=MESH)
    pl.semaphore_wait(barrier, len(others))


def offsets(n):
    order = []
    for d in range(1, n // 2 + 1):
        order.append(d)
        if n - d != d:
            order.append(n - d)
    return order


def gather_kernel(
    b_ref, c_ref, full, full_c,
    send_z, recv_z, send_a, recv_a, send_b, recv_b, send_a2, recv_a2,
    send_b2, recv_b2, send_s, recv_s, send_c, recv_c,
):
    x, z, y, c = place()
    g = (y % 2) * NC + c
    half = NZ // 2
    sibling = device(x, z, y, 1 - c)
    across = device(x, z, y + 1 - 2 * (y % 2), c)

    full[x, z, y, c] = b_ref[pl.ds(pl.multiple_of(g * PIECE, PIECE), PIECE), :]
    full_c[g] = c_ref[...]

    others = [device(x, (z + d) % NZ, y, c) for d in range(1, NZ)]
    others += [device((x + d) % NX, z, y, c) for d in range(1, NX)]
    others += [device(x, z, (y + d) % NY, c) for d in range(1, NY)]
    others += [sibling]
    greet(others)

    sent = []

    def send(source, send_sem, recv_sem, target):
        copy = pltpu.make_async_remote_copy(
            src_ref=source, dst_ref=source, send_sem=send_sem, recv_sem=recv_sem,
            device_id=target, device_id_type=MESH,
        )
        copy.start()
        sent.append(copy)

    def arrived(target, send_sem, recv_sem):
        pltpu.make_async_remote_copy(
            src_ref=target, dst_ref=target, send_sem=send_sem, recv_sem=recv_sem,
            device_id=sibling, device_id_type=MESH,
        ).wait_recv()

    passed = []

    def share(block, other_block):
        n = len(passed)
        send(block, send_s.at[n], recv_s.at[n], sibling)
        passed.append(other_block)

    for d in offsets(NZ):
        send(full.at[x, z, y, c], send_z.at[d - 1], recv_z.at[d - 1], device(x, (z + d) % NZ, y, c))
    send(full_c.at[g], send_c.at[0], recv_c.at[0], across)
    send(full_c.at[g], send_c.at[1], recv_c.at[1], sibling)
    for d in offsets(NZ):
        arrived(full.at[x, (z - d + NZ) % NZ, y, c], send_z.at[d - 1], recv_z.at[d - 1])

    lower, upper = pl.ds(0, half), pl.ds(half, half)
    for d in offsets(NX):
        send(full.at[x, lower, y, c], send_a.at[d - 1], recv_a.at[d - 1], device((x + d) % NX, z, y, c))
    for d in offsets(NY):
        send(full.at[x, upper, y, c], send_b.at[d - 1], recv_b.at[d - 1], device(x, z, (y + d) % NY, c))
    share(full.at[x, :, y, c], full.at[x, :, y, 1 - c])
    g_across = g + 2 - 4 * (y % 2)
    arrived(full_c.at[g_across], send_c.at[0], recv_c.at[0])
    send(full_c.at[g_across], send_c.at[2], recv_c.at[2], sibling)
    for d in offsets(NX):
        arrived(full.at[x, lower, y, c], send_a.at[d - 1], recv_a.at[d - 1])
    for d in offsets(NY):
        send(full.at[:, lower, y, c], send_a2.at[d - 1], recv_a2.at[d - 1], device(x, z, (y + d) % NY, c))
    for d in offsets(NX):
        xd = (x - d + NX) % NX
        share(full.at[xd, lower, y, c], full.at[xd, lower, y, 1 - c])
    for d in offsets(NY):
        arrived(full.at[x, upper, y, c], send_b.at[d - 1], recv_b.at[d - 1])
    for d in offsets(NX):
        send(full.at[x, upper, :, c], send_b2.at[d - 1], recv_b2.at[d - 1], device((x + d) % NX, z, y, c))
    for d in offsets(NY):
        yd = (y - d + NY) % NY
        share(full.at[x, upper, yd, c], full.at[x, upper, yd, 1 - c])
    for d in offsets(NY):
        yd = (y - d + NY) % NY
        arrived(full.at[:, lower, yd, c], send_a2.at[d - 1], recv_a2.at[d - 1])
        share(full.at[:, lower, yd, c], full.at[:, lower, yd, 1 - c])
    for d in offsets(NX):
        xd = (x - d + NX) % NX
        arrived(full.at[xd, upper, :, c], send_b2.at[d - 1], recv_b2.at[d - 1])
        share(full.at[xd, upper, :, c], full.at[xd, upper, :, 1 - c])
    for n, block in enumerate(passed):
        arrived(block, send_s.at[n], recv_s.at[n])
    arrived(full_c.at[0], send_c.at[1], recv_c.at[1])
    arrived(full_c.at[0], send_c.at[2], recv_c.at[2])
    for copy in sent:
        copy.wait_send()


def terms_kernel(
    counts_ref, row_ref, col_ref, depth_ref, b_ref, own_c_ref, c_ref, values_ref,
    partial_ref, inverse_ref, weights, work,
):
    partial_ref[...] = jnp.zeros_like(partial_ref)
    weights[...] = jnp.zeros_like(weights)
    live = counts_ref[0, 0]
    chunks = EDGE * EDGE // R

    def slot_step(s, carry):
        depth = pl.multiple_of(depth_ref[0, 0, s] * EDGE, EDGE)
        rows = own_c_ref[pl.ds(depth, EDGE), :]
        for q in range(4):
            weights[q, q * EDGE:(q + 1) * EDGE, :] = rows
        b_rows = b_ref[col_ref[0, 0, s]].astype(F32)
        cube = jnp.concatenate(
            [values_ref[0, 0, s, :, t * R:(t + 1) * R] for t in range(chunks)], axis=0
        )
        term = jnp.zeros((EDGE, R), F32)
        for q in range(4):
            product = jnp.dot(cube, weights[q], preferred_element_type=F32)
            for t in range(chunks):
                j = t * 4 + q
                term += product[t * EDGE:(t + 1) * EDGE, :] * b_rows[j:j + 1, :]
        row = jnp.full((EDGE, R), row_ref[0, 0, s], jnp.int32)
        term = jnp.where(jnp.full((EDGE, R), live - s, jnp.int32) > 0, term, 0.0)
        for i in range(2):
            partial_ref[i * EDGE:(i + 1) * EDGE, :] += jnp.where(row == i, term, 0.0)
        return carry

    lax.fori_loop(0, NB, slot_step, 0)

    def gram(ref_at, parts):
        def step(i, total):
            block = ref_at(i)
            return total + lax.dot_general(
                block, block, (((0,), (0,)), ((), ())), preferred_element_type=F32
            )
        return lax.fori_loop(0, parts, step, jnp.zeros((R, R), F32))

    gram_b = gram(lambda i: b_ref[pl.ds(i * 8, 8)].reshape(8 * EDGE, R), NX * NZ * YH // 8)
    gram_c = gram(lambda i: c_ref[i], 4)
    invert(gram_b * gram_c, inverse_ref, work)


def split(a):
    high = a.astype(BF16)
    return high, (a - high.astype(F32)).astype(BF16)


def three_pass(a, b):
    a_high, a_low = a
    b_high, b_low = b
    return jnp.dot(
        jnp.concatenate([a_high, a_low, a_high], axis=1),
        jnp.concatenate([b_high, b_high, b_low], axis=0),
        preferred_element_type=F32,
    )


def exact_dot(a, b):
    return jnp.dot(a, b, precision=lax.Precision.HIGHEST, preferred_element_type=F32)


def invert(system, out_ref, work):
    sub = lax.broadcasted_iota(jnp.int32, (R, R), 0)
    lane = lax.broadcasted_iota(jnp.int32, (R, R), 1)
    eye = jnp.where(sub == lane, 1.0, 0.0).astype(F32)
    diagonal = system * eye
    across = lax.rsqrt(jnp.sum(diagonal, axis=0, keepdims=True))
    down = lax.rsqrt(jnp.sum(diagonal, axis=1, keepdims=True))
    scaled = system * across * down
    bound = jnp.max(jnp.sum(jnp.abs(scaled), axis=0, keepdims=True), axis=1, keepdims=True)
    start = 1.0 / bound
    rest = eye - scaled * start
    guess = (eye + rest) * start
    for _ in range(8):
        rest_parts = split(rest)
        rest = three_pass(rest_parts, rest_parts)
        guess = guess + three_pass(split(guess), split(rest))
    work[...] = guess

    def unfinished(state):
        count, error = state
        return jnp.logical_and(count < 24, jnp.logical_not(error <= 2e-4))

    def refine(state):
        count, _ = state
        guess = work[...]
        rest = eye - exact_dot(guess, scaled)
        work[...] = guess + exact_dot(guess, rest)
        error = jnp.max(jnp.sum(jnp.abs(rest), axis=0, keepdims=True))
        return count + 1, error

    _, error = lax.while_loop(unfinished, refine, (jnp.int32(0), jnp.float32(1.0)))

    @pl.when(jnp.logical_not(error <= 2e-4))
    def _():
        work[...] = scaled

        def pivot(k, carry):
            a = work[...]
            row = work[pl.ds(k, 1), :]
            column = jnp.sum(jnp.where(lane == k, a, 0.0), axis=1, keepdims=True)
            value = jnp.sum(jnp.where(lane[:1] == k, row, 0.0), axis=1, keepdims=True)
            row = row / value
            updated = jnp.where(lane == k, -column / value, a - column * row)
            updated = jnp.where(sub == k, jnp.where(lane == k, 1.0 / value, row), updated)
            work[...] = updated
            return carry

        lax.fori_loop(0, R, pivot, 0)

    out_ref[...] = work[...] * across * down


def update_kernel(
    partial_ref, inverse_ref, a_ref, full, parts,
    send_g, recv_g, send_z, recv_z, send_a, recv_a, send_b, recv_b,
    send_a2, recv_a2, send_b2, recv_b2,
):
    x, z, y, c = place()
    yh, yl = y // 2, y % 2
    g = yl * NC + c
    half = NZ // 2
    facing = device(x, z, (y + 2) % NY, c)

    def member(other):
        return device(x, z, yh * 2 + other // NC, other % NC)

    others = [member((g + d) % 4) for d in range(1, 4)]
    others += [device(x, (z + d) % NZ, y, c) for d in range(1, NZ)]
    others += [device((x + d) % NX, z, y, c) for d in range(1, NX)]
    others += [facing]
    greet(others)

    sent = []

    def send(source, target, send_sem, recv_sem, other):
        copy = pltpu.make_async_remote_copy(
            src_ref=source, dst_ref=target, send_sem=send_sem, recv_sem=recv_sem,
            device_id=other, device_id_type=MESH,
        )
        copy.start()
        sent.append(copy)

    def arrived(target, send_sem, recv_sem):
        pltpu.make_async_remote_copy(
            src_ref=target, dst_ref=target, send_sem=send_sem, recv_sem=recv_sem,
            device_id=facing, device_id_type=MESH,
        ).wait_recv()

    def own(other):
        return pl.ds(pl.multiple_of(other * ROWS, ROWS), ROWS)

    for d in (2, 1, 3):
        other = (g + d) % 4
        send(partial_ref.at[own(other)], parts.at[d - 1], send_g.at[d - 1], recv_g.at[d - 1], member(other))
    total = partial_ref[own(g), :]
    for d in (1, 3, 2):
        arrived(parts.at[d - 1], send_g.at[d - 1], recv_g.at[d - 1])
        total = total + parts[d - 1]
    solved = exact_dot(total, inverse_ref[...]).astype(BF16)
    a_ref[...] = solved
    full[x, z, yh] = solved

    for d in offsets(NZ):
        here = full.at[x, z, yh]
        send(here, here, send_z.at[d - 1], recv_z.at[d - 1], device(x, (z + d) % NZ, y, c))
    for d in offsets(NZ):
        arrived(full.at[x, (z - d + NZ) % NZ, yh], send_z.at[d - 1], recv_z.at[d - 1])
    lower, upper = pl.ds(0, half), pl.ds(half, half)
    for d in offsets(NX):
        here = full.at[x, lower, yh]
        send(here, here, send_a.at[d - 1], recv_a.at[d - 1], device((x + d) % NX, z, y, c))
    here = full.at[x, upper, yh]
    send(here, here, send_b.at[0], recv_b.at[0], facing)
    for d in offsets(NX):
        arrived(full.at[x, lower, yh], send_a.at[d - 1], recv_a.at[d - 1])
    here = full.at[:, lower, yh]
    send(here, here, send_a2.at[0], recv_a2.at[0], facing)
    arrived(full.at[x, upper, yh], send_b.at[0], recv_b.at[0])
    for d in offsets(NX):
        here = full.at[x, upper]
        send(here, here, send_b2.at[d - 1], recv_b2.at[d - 1], device((x + d) % NX, z, y, c))
    arrived(full.at[:, lower, yh], send_a2.at[0], recv_a2.at[0])
    for d in offsets(NX):
        arrived(full.at[x, upper], send_b2.at[d - 1], recv_b2.at[d - 1])
    for copy in sent:
        copy.wait_send()


def pick_kernel(fetch_ref, full, fetched_ref, units):
    def pick(s, carry):
        f = fetch_ref[0, 0, s]
        owner, within = lax.div(f, 2), lax.rem(f, 2)
        start = pl.multiple_of(within * PIECE, PIECE)
        pair = lax.div(owner, YH)
        unit = full[lax.div(pair, NZ), lax.rem(pair, NZ), lax.rem(owner, YH), pl.ds(start, PIECE), :]
        unit = unit.astype(F32)
        for h in range(2):
            units[h, pl.ds(pl.multiple_of(s * PIECE, PIECE), PIECE), :] = unit[:, h * 128:(h + 1) * 128]
        return carry

    lax.fori_loop(0, SLOTS, pick, 0, unroll=4)
    for r in range(PIECE):
        for h in range(2):
            at = r * R + h * 128
            picked = units.at[h][pl.ds(r, SLOTS, stride=PIECE), :]
            fetched_ref[0, 0, :, at:at + 128] = picked.astype(BF16)


def dma(n):
    return pltpu.SemaphoreType.DMA((n,))


VMEM = pl.BlockSpec(memory_space=pltpu.VMEM)
SMEM = pl.BlockSpec(memory_space=pltpu.SMEM)
ANY = pl.BlockSpec(memory_space=pl.ANY)


def on_device(values, counts, row_block, col_block, depth_block, factor_b, factor_c, fetch_list):
    full_b, full_c = pl.pallas_call(
        gather_kernel,
        out_shape=(
            jax.ShapeDtypeStruct((NX, NZ, NY, NC, PIECE, R), BF16),
            jax.ShapeDtypeStruct((4, 256, R), BF16),
        ),
        in_specs=[VMEM] * 2,
        out_specs=(VMEM, VMEM),
        scratch_shapes=[
            dma(NZ - 1), dma(NZ - 1), dma(NX - 1), dma(NX - 1), dma(NY - 1), dma(NY - 1),
            dma(NY - 1), dma(NY - 1), dma(NX - 1), dma(NX - 1), dma(13), dma(13),
            dma(3), dma(3),
        ],
        compiler_params=pltpu.CompilerParams(
            collective_id=0, has_side_effects=True, vmem_limit_bytes=12 << 20
        ),
        name="gather_factors",
    )(factor_b, factor_c)
    partial, inverse = pl.pallas_call(
        terms_kernel,
        out_shape=(
            jax.ShapeDtypeStruct((2 * EDGE, R), F32),
            jax.ShapeDtypeStruct((R, R), F32),
        ),
        in_specs=[SMEM] * 4 + [VMEM] * 4,
        out_specs=(VMEM, VMEM),
        scratch_shapes=[pltpu.VMEM((4, R, R), BF16), pltpu.VMEM((R, R), F32)],
        compiler_params=pltpu.CompilerParams(vmem_limit_bytes=32 << 20),
        name="terms_inverse",
    )(counts, row_block, col_block, depth_block,
      full_b.reshape(NX * NZ * YH, EDGE, R), factor_c, full_c, values)
    a_new, full_a = pl.pallas_call(
        update_kernel,
        out_shape=(
            jax.ShapeDtypeStruct((ROWS, R), BF16),
            jax.ShapeDtypeStruct((NX, NZ, YH, ROWS, R), BF16),
        ),
        in_specs=[VMEM, VMEM],
        out_specs=(VMEM, VMEM),
        scratch_shapes=[
            pltpu.VMEM((3, ROWS, R), F32),
            dma(3), dma(3), dma(NZ - 1), dma(NZ - 1), dma(NX - 1), dma(NX - 1), dma(1), dma(1),
            dma(1), dma(1), dma(NX - 1), dma(NX - 1),
        ],
        compiler_params=pltpu.CompilerParams(
            collective_id=1, has_side_effects=True, vmem_limit_bytes=12 << 20
        ),
        name="update_gather",
    )(partial, inverse)
    fetched = pl.pallas_call(
        pick_kernel,
        out_shape=jax.ShapeDtypeStruct((1, 1, SLOTS, PIECE * R), BF16),
        in_specs=[SMEM, VMEM],
        out_specs=VMEM,
        scratch_shapes=[pltpu.VMEM((2, SLOTS * PIECE, 128), F32)],
        compiler_params=pltpu.CompilerParams(vmem_limit_bytes=16 << 20),
        name="pick_units",
    )(fetch_list, full_a)
    return a_new, fetched


def solution(mesh):
    placed = (
        P("blk", "grp", None, None, None),
        P("blk", "grp"),
        P("blk", "grp", None),
        P("blk", "grp", None),
        P("blk", "grp", None),
        P("blk", None),
        P("grp", None),
        P("blk", "grp", None),
    )
    return jax.shard_map(
        on_device,
        mesh=mesh,
        in_specs=placed,
        out_specs=(P(("blk", "grp"), None), P("blk", "grp", None, None)),
        check_vma=False,
    )
```

```python
import functools

import jax
import jax.numpy as jnp
from jax import lax
from jax.experimental import pallas as pl
from jax.experimental.pallas import tpu as pltpu
from jax.sharding import PartitionSpec as P

MESH = pl.DeviceIdType.MESH
NX, NZ, NY, NC = 4, 16, 4, 2
YH = 2
R = 256
EDGE = 64
NB = 6
PIECE = 16
ROWS = 32
SLOTS = 64
F32 = jnp.float32
BF16 = jnp.bfloat16


def place():
    b, g = lax.axis_index("blk"), lax.axis_index("grp")
    x, z, yh = b // (NZ * YH), (b // YH) % NZ, b % YH
    return x, z, yh * 2 + g // NC, g % NC


def device(x, z, y, c):
    return ((x * NZ + z) * YH + y // 2, (y % 2) * NC + c)


def greet(others):
    barrier = pltpu.get_barrier_semaphore()
    for other in others:
        pl.semaphore_signal(barrier, inc=1, device_id=other, device_id_type=MESH)
    pl.semaphore_wait(barrier, len(others))


def slot_of(d):
    d = d % NZ
    return max(2 * d - 1, 0) if d <= NZ // 2 else 2 * (NZ - d)


def slot_at(z_there, z_here):
    d = lax.rem(z_there - z_here + NZ, NZ)
    return jnp.where(d <= NZ // 2, jnp.maximum(2 * d - 1, 0), 2 * (NZ - d))


def groups():
    return [(0, 1)] + [(i, 2) for i in range(1, NZ - 1, 2)] + [(NZ - 1, 1)]


def offsets(n):
    order = []
    for d in range(1, n // 2 + 1):
        order.append(d)
        if n - d != d:
            order.append(n - d)
    return order


class Mover:
    def __init__(self, other):
        self.sent, self.other = [], other

    def send(self, source, target, send_sem, recv_sem, device_id):
        copy = pltpu.make_async_remote_copy(
            src_ref=source, dst_ref=target, send_sem=send_sem, recv_sem=recv_sem,
            device_id=device_id, device_id_type=MESH,
        )
        copy.start()
        self.sent.append(copy)

    def arrived(self, target, send_sem, recv_sem):
        pltpu.make_async_remote_copy(
            src_ref=target, dst_ref=target, send_sem=send_sem, recv_sem=recv_sem,
            device_id=self.other, device_id_type=MESH,
        ).wait_recv()

    def finish(self):
        for copy in self.sent:
            copy.wait_send()


LAGS_B = (1, 2, 3)
LAGS_A = (1, 2)
X_FIRST_B = (1, 3, 5, 7)
X_FIRST_A = (1, 2, 4, 5, 7)


def gather_kernel(
    b_ref, c_ref, values_ref,
    full, own_c, cubes, system_ref,
    full_c,
    local_sem, send_z, recv_z, send_1, recv_1, send_2, recv_2, send_s, recv_s, send_c, recv_c,
):
    x, z, y, c = place()
    g = (y % 2) * NC + c
    sibling = device(x, z, y, 1 - c)
    across = device(x, z, y + 1 - 2 * (y % 2), c)
    own_rows = pl.ds(pl.multiple_of(g * PIECE, PIECE), PIECE)
    loads = [
        pltpu.make_async_copy(b_ref.at[own_rows], full.at[x, 0, y, c], local_sem.at[0]),
        pltpu.make_async_copy(c_ref, own_c, local_sem.at[1]),
        pltpu.make_async_copy(values_ref.at[0, 0], cubes, local_sem.at[2]),
    ]
    for load in loads:
        load.start()

    others = [device(x, (z + d) % NZ, y, c) for d in range(1, NZ)]
    others += [device((x + d) % NX, z, y, c) for d in range(1, NX)]
    others += [device(x, z, (y + d) % NY, c) for d in range(1, NY)]
    others += [sibling]
    loads[0].wait()
    loads[1].wait()
    greet(others)
    mover = Mover(sibling)
    send, arrived = mover.send, mover.arrived

    for d in offsets(NZ):
        send(
            full.at[x, 0, y, c], full.at[x, slot_of(-d), y, c],
            send_z.at[d - 1], recv_z.at[d - 1], device(x, (z + d) % NZ, y, c),
        )

    def first(k, start, size):
        for slot in range(start, start + size):
            for d in range(1, NZ):
                if slot_of(-d) == slot:
                    arrived(full.at[x, slot, y, c], send_z.at[d - 1], recv_z.at[d - 1])
        here = full.at[x, pl.ds(start, size), y, c]
        for d in offsets(4):
            there = device((x + d) % NX, z, y, c) if k in X_FIRST_B else device(x, z, (y + d) % NY, c)
            send(here, here, send_1.at[k, d - 1], recv_1.at[k, d - 1], there)

    def second(k, start, size):
        for d in offsets(4):
            arrived(full.at[x, pl.ds(start, size), y, c], send_1.at[k, d - 1], recv_1.at[k, d - 1])
        if k in X_FIRST_B:
            here = full.at[:, pl.ds(start, size), y, c]
        else:
            here = full.at[x, pl.ds(start, size), :, c]
        for d in offsets(4):
            there = device(x, z, (y + d) % NY, c) if k in X_FIRST_B else device((x + d) % NX, z, y, c)
            send(here, here, send_2.at[k, d - 1], recv_2.at[k, d - 1], there)

    def third(k, start, size):
        for d in offsets(4):
            arrived(full.at[:, pl.ds(start, size), y, c], send_2.at[k, d - 1], recv_2.at[k, d - 1])
        here = full.at[:, pl.ds(start, size), :, c]
        send(here, here, send_s.at[k], recv_s.at[k], sibling)

    grams = [jnp.zeros((R, R), F32)]

    def gram(block):
        return lax.dot_general(
            block, block, (((0,), (0,)), ((), ())), preferred_element_type=F32
        )

    def fourth(k, start, size):
        arrived(full.at[:, pl.ds(start, size), :, 1 - c], send_s.at[k], recv_s.at[k])
        for i in range(NX):
            block = full[i, start:start + size].reshape(size * NY * NC * PIECE, R)
            grams[0] = grams[0] + gram(block)

    parts = groups()
    stages = (first, second, third, fourth)
    lags = (0,) + LAGS_B
    for t in range(len(parts) + lags[-1]):
        for stage, lag in zip(stages, lags):
            if 0 <= t - lag < len(parts):
                stage(t - lag, *parts[t - lag])
        if t == 0:
            send(own_c, full_c.at[g], send_c.at[0], recv_c.at[0], across)
            send(own_c, full_c.at[g], send_c.at[1], recv_c.at[1], sibling)
            g_across = g + 2 - 4 * (y % 2)
            gram_c = gram(own_c[...])
        if t == 3:
            arrived(full_c.at[g_across], send_c.at[0], recv_c.at[0])
            send(full_c.at[g_across], full_c.at[g_across], send_c.at[2], recv_c.at[2], sibling)
            gram_c = gram_c + gram(full_c[g_across])
    for i, other in ((1, g + 1 - 2 * c), (2, g_across + 1 - 2 * c)):
        arrived(full_c.at[other], send_c.at[i], recv_c.at[i])
        gram_c = gram_c + gram(full_c[other])
    system_ref[...] = grams[0] * gram_c
    loads[2].wait()
    mover.finish()


def split(a):
    high = a.astype(BF16)
    return high, (a - high.astype(F32)).astype(BF16)


def three_pass(a, b):
    a_high, a_low = a
    b_high, b_low = b
    return jnp.dot(
        jnp.concatenate([a_high, a_low, a_high], axis=1),
        jnp.concatenate([b_high, b_high, b_low], axis=0),
        preferred_element_type=F32,
    )


def exact_dot(a, b):
    return jnp.dot(a, b, precision=lax.Precision.HIGHEST, preferred_element_type=F32)


def invert(system, out_ref, work):
    sub = lax.broadcasted_iota(jnp.int32, (R, R), 0)
    lane = lax.broadcasted_iota(jnp.int32, (R, R), 1)
    eye = jnp.where(sub == lane, 1.0, 0.0).astype(F32)
    diagonal = system * eye
    across = lax.rsqrt(jnp.sum(diagonal, axis=0, keepdims=True))
    down = lax.rsqrt(jnp.sum(diagonal, axis=1, keepdims=True))
    scaled = system * across * down
    bound = jnp.max(jnp.sum(jnp.abs(scaled), axis=0, keepdims=True), axis=1, keepdims=True)
    start = 1.0 / bound
    rest = eye - scaled * start
    guess = (eye + rest) * start
    for _ in range(7):
        rest_parts = split(rest)
        rest = three_pass(rest_parts, rest_parts)
        guess = guess + three_pass(split(rest), split(guess))
    work[...] = guess

    def unfinished(state):
        count, error = state
        return jnp.logical_and(count < 24, jnp.logical_not(error <= 1e-3))

    def refine(state):
        count, _ = state
        guess = work[...]
        rest = eye - exact_dot(guess, scaled)
        work[...] = guess + exact_dot(rest, guess)
        error = jnp.max(jnp.sum(jnp.abs(rest), axis=0, keepdims=True))
        return count + 1, error

    _, error = lax.while_loop(unfinished, refine, (jnp.int32(0), jnp.float32(1.0)))

    @pl.when(jnp.logical_not(error <= 1e-3))
    def _():
        work[...] = scaled

        def pivot(k, carry):
            a = work[...]
            row = work[pl.ds(k, 1), :]
            column = jnp.sum(jnp.where(lane == k, a, 0.0), axis=1, keepdims=True)
            value = jnp.sum(jnp.where(lane[:1] == k, row, 0.0), axis=1, keepdims=True)
            row = row / value
            updated = jnp.where(lane == k, -column / value, a - column * row)
            updated = jnp.where(sub == k, jnp.where(lane == k, 1.0 / value, row), updated)
            work[...] = updated
            return carry

        lax.fori_loop(0, R, pivot, 0)

    out_ref[...] = work[...] * across * down


def inverse_kernel(
    counts_ref, row_ref, col_ref, depth_ref, full_ref, c_ref, system_ref,
    inverse_ref, rows_b_ref, rows_c_ref, keep_ref, work,
):
    z = place()[1]
    live = counts_ref[0, 0]
    for s in range(NB):
        col = col_ref[0, 0, s]
        pair = lax.div(col, YH)
        slot = slot_at(lax.rem(pair, NZ), z)
        rows = full_ref[lax.div(pair, NZ), slot, pl.ds(lax.rem(col, YH) * 2, 2)]
        rows_b_ref[s] = rows.reshape(EDGE, R).astype(F32)
        depth = pl.multiple_of(depth_ref[0, 0, s] * EDGE, EDGE)
        rows_c_ref[s] = c_ref[pl.ds(depth, EDGE), :]
        for i in range(2):
            keep = jnp.logical_and(s < live, row_ref[0, 0, s] == i)
            keep_ref[s, i] = jnp.full((8, R), jnp.where(keep, 1, 0), jnp.int32)
    invert(system_ref[...], inverse_ref, work)


def update_kernel(
    cubes, rows_b_ref, rows_c_ref, keep_ref, inverse_ref,
    a_ref, full,
    partial, weights, parts,
    send_g, recv_g, send_z, recv_z, send_1, recv_1, send_2, recv_2,
):
    x, z, y, c = place()
    yh, yl = y // 2, y % 2
    g = yl * NC + c
    facing = device(x, z, (y + 2) % NY, c)

    def member(other):
        return device(x, z, yh * 2 + other // NC, other % NC)

    others = [member((g + d) % 4) for d in range(1, 4)]
    others += [device(x, (z + d) % NZ, y, c) for d in range(1, NZ)]
    others += [device((x + d) % NX, z, y, c) for d in range(1, NX)]
    others += [facing]
    barrier = pltpu.get_barrier_semaphore()
    for other in others:
        pl.semaphore_signal(barrier, inc=1, device_id=other, device_id_type=MESH)

    partial[...] = jnp.zeros_like(partial)
    weights[...] = jnp.zeros_like(weights)
    chunks = EDGE * EDGE // R

    def slot_step(s, carry):
        for q in range(4):
            weights[q, q * EDGE:(q + 1) * EDGE, :] = rows_c_ref[s]
        b_rows = rows_b_ref[s]
        cube = jnp.concatenate(
            [cubes[s, :, t * R:(t + 1) * R] for t in range(chunks)], axis=0
        )
        term = jnp.zeros((EDGE, R), F32)
        for q in range(4):
            product = jnp.dot(cube, weights[q], preferred_element_type=F32)
            for t in range(chunks):
                j = t * 4 + q
                term += product[t * EDGE:(t + 1) * EDGE, :] * b_rows[j:j + 1, :]
        for i in range(2):
            keep = keep_ref[s, i][:1, :] > 0
            partial[i * EDGE:(i + 1) * EDGE, :] += jnp.where(keep, term, 0.0)
        return carry

    lax.fori_loop(0, NB, slot_step, 0)

    pl.semaphore_wait(barrier, len(others))
    mover = Mover(facing)
    send, arrived = mover.send, mover.arrived

    def own(other):
        return pl.ds(pl.multiple_of(other * ROWS, ROWS), ROWS)

    for d in (2, 1, 3):
        other = (g + d) % 4
        send(partial.at[own(other)], parts.at[d - 1], send_g.at[d - 1], recv_g.at[d - 1], member(other))
    total = partial[own(g), :]
    for d in (1, 3, 2):
        arrived(parts.at[d - 1], send_g.at[d - 1], recv_g.at[d - 1])
        total = total + parts[d - 1]
    solved = exact_dot(total, inverse_ref[...]).astype(BF16)
    a_ref[...] = solved
    full[x, 0, yh] = solved

    for d in offsets(NZ):
        send(
            full.at[x, 0, yh], full.at[x, slot_of(-d), yh],
            send_z.at[d - 1], recv_z.at[d - 1], device(x, (z + d) % NZ, y, c),
        )

    def first(k, start, size):
        for slot in range(start, start + size):
            for d in range(1, NZ):
                if slot_of(-d) == slot:
                    arrived(full.at[x, slot, yh], send_z.at[d - 1], recv_z.at[d - 1])
        here = full.at[x, pl.ds(start, size), yh]
        if k in X_FIRST_A:
            for d in offsets(NX):
                send(here, here, send_1.at[k, d - 1], recv_1.at[k, d - 1], device((x + d) % NX, z, y, c))
        else:
            send(here, here, send_1.at[k, 0], recv_1.at[k, 0], facing)

    def second(k, start, size):
        here = full.at[x, pl.ds(start, size), yh]
        if k in X_FIRST_A:
            for d in offsets(NX):
                arrived(here, send_1.at[k, d - 1], recv_1.at[k, d - 1])
            column = full.at[:, pl.ds(start, size), yh]
            send(column, column, send_2.at[k, 0], recv_2.at[k, 0], facing)
        else:
            arrived(here, send_1.at[k, 0], recv_1.at[k, 0])
            both = full.at[x, pl.ds(start, size)]
            for d in offsets(NX):
                send(both, both, send_2.at[k, d - 1], recv_2.at[k, d - 1], device((x + d) % NX, z, y, c))

    def third(k, start, size):
        if k in X_FIRST_A:
            arrived(full.at[:, pl.ds(start, size), yh], send_2.at[k, 0], recv_2.at[k, 0])
        else:
            for d in offsets(NX):
                arrived(full.at[x, pl.ds(start, size)], send_2.at[k, d - 1], recv_2.at[k, d - 1])

    order = groups()
    stages = (first, second, third)
    lags = (0, LAGS_A[0], LAGS_A[1])
    for t in range(len(order) + lags[-1]):
        for stage, lag in zip(stages, lags):
            if 0 <= t - lag < len(order):
                stage(t - lag, *order[t - lag])
    mover.finish()


def pick_kernel(fetch_ref, full, fetched_ref, units):
    z = place()[1]

    def pick(s, carry):
        f = fetch_ref[0, 0, s]
        owner, within = lax.div(f, 2), lax.rem(f, 2)
        start = pl.multiple_of(within * PIECE, PIECE)
        pair = lax.div(owner, YH)
        slot = slot_at(lax.rem(pair, NZ), z)
        unit = full[lax.div(pair, NZ), slot, lax.rem(owner, YH), pl.ds(start, PIECE), :]
        unit = unit.astype(F32)
        for h in range(2):
            units[h, pl.ds(pl.multiple_of(s * PIECE, PIECE), PIECE), :] = unit[:, h * 128:(h + 1) * 128]
        return carry

    lax.fori_loop(0, SLOTS, pick, 0, unroll=4)
    for r in range(PIECE):
        for h in range(2):
            at = r * R + h * 128
            picked = units.at[h][pl.ds(r, SLOTS, stride=PIECE), :]
            fetched_ref[0, 0, :, at:at + 128] = picked.astype(BF16)


def dma(*shape):
    return pltpu.SemaphoreType.DMA(shape)


VMEM = pl.BlockSpec(memory_space=pltpu.VMEM)
SMEM = pl.BlockSpec(memory_space=pltpu.SMEM)
ANY = pl.BlockSpec(memory_space=pl.ANY)


def on_device(values, counts, row_block, col_block, depth_block, factor_b, factor_c, fetch_list):
    n_groups = len(groups())
    full_b, own_c, cubes, system = pl.pallas_call(
        gather_kernel,
        out_shape=(
            jax.ShapeDtypeStruct((NX, NZ, NY, NC, PIECE, R), BF16),
            jax.ShapeDtypeStruct((R, R), BF16),
            jax.ShapeDtypeStruct((NB, EDGE, EDGE * EDGE), BF16),
            jax.ShapeDtypeStruct((R, R), F32),
        ),
        in_specs=[ANY] * 3,
        out_specs=(VMEM,) * 4,
        scratch_shapes=[
            pltpu.VMEM((4, R, R), BF16),
            dma(3), dma(NZ - 1), dma(NZ - 1), dma(n_groups, 3), dma(n_groups, 3),
            dma(n_groups, 3), dma(n_groups, 3), dma(n_groups), dma(n_groups), dma(3), dma(3),
        ],
        compiler_params=pltpu.CompilerParams(
            collective_id=0, has_side_effects=True, vmem_limit_bytes=24 << 20
        ),
        name="gather_factors",
    )(factor_b, factor_c, values)
    inverse, rows_b, rows_c, keep = pl.pallas_call(
        inverse_kernel,
        out_shape=(
            jax.ShapeDtypeStruct((R, R), F32),
            jax.ShapeDtypeStruct((NB, EDGE, R), F32),
            jax.ShapeDtypeStruct((NB, EDGE, R), BF16),
            jax.ShapeDtypeStruct((NB, 2, 8, R), jnp.int32),
        ),
        in_specs=[SMEM] * 4 + [VMEM] * 3,
        out_specs=(VMEM,) * 4,
        scratch_shapes=[pltpu.VMEM((R, R), F32)],
        compiler_params=pltpu.CompilerParams(vmem_limit_bytes=24 << 20),
        name="invert_select",
    )(counts, row_block, col_block, depth_block, full_b, own_c, system)
    a_new, full_a = pl.pallas_call(
        update_kernel,
        out_shape=(
            jax.ShapeDtypeStruct((ROWS, R), BF16),
            jax.ShapeDtypeStruct((NX, NZ, YH, ROWS, R), BF16),
        ),
        in_specs=[VMEM] * 5,
        out_specs=(VMEM, VMEM),
        scratch_shapes=[
            pltpu.VMEM((2 * EDGE, R), F32),
            pltpu.VMEM((4, R, R), BF16),
            pltpu.VMEM((3, ROWS, R), F32),
            dma(3), dma(3), dma(NZ - 1), dma(NZ - 1), dma(n_groups, 3), dma(n_groups, 3),
            dma(n_groups, 3), dma(n_groups, 3),
        ],
        compiler_params=pltpu.CompilerParams(
            collective_id=1, has_side_effects=True, vmem_limit_bytes=24 << 20
        ),
        name="update_gather",
    )(cubes, rows_b, rows_c, keep, inverse)
    fetched = pl.pallas_call(
        pick_kernel,
        out_shape=jax.ShapeDtypeStruct((1, 1, SLOTS, PIECE * R), BF16),
        in_specs=[SMEM, VMEM],
        out_specs=VMEM,
        scratch_shapes=[pltpu.VMEM((2, SLOTS * PIECE, 128), F32)],
        compiler_params=pltpu.CompilerParams(vmem_limit_bytes=16 << 20),
        name="pick_units",
    )(fetch_list, full_a)
    return a_new, fetched


def solution(mesh):
    placed = (
        P("blk", "grp", None, None, None),
        P("blk", "grp"),
        P("blk", "grp", None),
        P("blk", "grp", None),
        P("blk", "grp", None),
        P("blk", None),
        P("grp", None),
        P("blk", "grp", None),
    )
    return jax.shard_map(
        on_device,
        mesh=mesh,
        in_specs=placed,
        out_specs=(P(("blk", "grp"), None), P("blk", "grp", None, None)),
        check_vma=False,
    )
```

```python
import functools

import jax
import jax.numpy as jnp
from jax import lax
from jax.experimental import pallas as pl
from jax.experimental.pallas import tpu as pltpu
from jax.sharding import PartitionSpec as P

MESH = pl.DeviceIdType.MESH
NX, NZ, NY, NC = 4, 16, 4, 2
YH = 2
R = 256
EDGE = 64
NB = 6
PIECE = 16
ROWS = 32
SLOTS = 64
F32 = jnp.float32
BF16 = jnp.bfloat16


def place():
    b, g = lax.axis_index("blk"), lax.axis_index("grp")
    x, z, yh = b // (NZ * YH), (b // YH) % NZ, b % YH
    return x, z, yh * 2 + g // NC, g % NC


def device(x, z, y, c):
    return ((x * NZ + z) * YH + y // 2, (y % 2) * NC + c)


def announce(others):
    barrier = pltpu.get_barrier_semaphore()
    for other in others:
        pl.semaphore_signal(barrier, inc=1, device_id=other, device_id_type=MESH)


def await_greetings(others):
    pl.semaphore_wait(pltpu.get_barrier_semaphore(), len(others))


def slot_at(z_there, z_here):
    d = lax.rem(z_here - z_there + NZ, NZ)
    left = d <= NZ // 2
    step = jnp.where(left, d, NZ - d) - 1
    slot = 4 * (step // 2) + step % 2 + jnp.where(left, 1, 3)
    return jnp.where(d == 0, 0, slot)


def groups():
    return [(0, 1)] + [(i, 2) for i in range(1, NZ - 1, 2)] + [(NZ - 1, 1)]


def offsets(n):
    order = []
    for d in range(1, n // 2 + 1):
        order.append(d)
        if n - d != d:
            order.append(n - d)
    return order


def schedule(gaps):
    events = []
    for k in range(len(groups())):
        time = (k + 1) // 2 * 2.2
        for stage in range(len(gaps) + 1):
            events.append((time + sum(gaps[:stage]), stage, k))
    return [event[1:] for event in sorted(events)]


class Mover:
    def __init__(self, other):
        self.sent, self.other = [], other

    def send(self, source, target, send_sem, recv_sem, device_id):
        copy = pltpu.make_async_remote_copy(
            src_ref=source, dst_ref=target, send_sem=send_sem, recv_sem=recv_sem,
            device_id=device_id, device_id_type=MESH,
        )
        copy.start()
        self.sent.append(copy)

    def arrived(self, target, send_sem, recv_sem):
        pltpu.make_async_remote_copy(
            src_ref=target, dst_ref=target, send_sem=send_sem, recv_sem=recv_sem,
            device_id=self.other, device_id_type=MESH,
        ).wait_recv()

    def finish(self):
        for copy in self.sent:
            copy.wait_send()


class Chain:
    def __init__(self, mover, at, send_sem, recv_sem, x, z, y, c):
        self.mover, self.at, self.send_sem, self.recv_sem = mover, at, send_sem, recv_sem
        self.place = x, z, y, c

    def peer(self, d):
        x, z, y, c = self.place
        return device(x, (z + d + NZ) % NZ, y, c)

    def start(self):
        for i, d in enumerate((1, 2, -1, -2)):
            self.mover.send(
                self.at(0, 1), self.at(1 + i, 1), self.send_sem.at[i], self.recv_sem.at[i], self.peer(d)
            )

    def arrive(self, k):
        order = groups()
        if k in (1, 2):
            for i in (2 * k - 2, 2 * k - 1):
                self.mover.arrived(self.at(1 + i, 1), self.send_sem.at[i], self.recv_sem.at[i])
        elif k > 2:
            self.mover.arrived(self.at(*order[k]), self.send_sem.at[k + 1], self.recv_sem.at[k + 1])
        if 1 <= k < len(order) - 2:
            start, size = order[k + 2]
            self.mover.send(
                self.at(order[k][0], size), self.at(start, size),
                self.send_sem.at[k + 3], self.recv_sem.at[k + 3], self.peer(2 if k % 2 else -2),
            )


GAPS_B = (2.3, 4.5, 2.2)
GAPS_A = (2.3, 4.5)
X_FIRST_B = (1, 3, 5, 7)
X_FIRST_A = (1, 2, 4, 5, 7)


def gather_kernel(
    b_ref, c_ref,
    full, own_c, system_ref,
    full_c,
    local_sem, send_z, recv_z, send_1, recv_1, send_2, recv_2, send_s, recv_s, send_c, recv_c,
):
    x, z, y, c = place()
    g = (y % 2) * NC + c
    sibling = device(x, z, y, 1 - c)
    g_across = g + 2 - 4 * (y % 2)

    def c_half(i):
        return pl.ds(i * R // 2, R // 2)

    own_rows = pl.ds(pl.multiple_of(g * PIECE, PIECE), PIECE)
    loads = [
        pltpu.make_async_copy(b_ref.at[own_rows], full.at[x, 0, y, c], local_sem.at[0]),
        pltpu.make_async_copy(c_ref, own_c, local_sem.at[1]),
    ]
    for load in loads:
        load.start()

    others = [device(x, (z + d + NZ) % NZ, y, c) for d in (1, 2, -1, -2)]
    others += [device((x + d) % NX, z, y, c) for d in range(1, NX)]
    others += [device(x, z, (y + d) % NY, c) for d in range(1, NY)]
    others += [sibling]
    announce(others)
    loads[0].wait()
    loads[1].wait()
    await_greetings(others)
    mover = Mover(sibling)
    chain = Chain(mover, lambda i, n: full.at[x, pl.ds(i, n), y, c], send_z, recv_z, x, z, y, c)
    send, arrived = mover.send, mover.arrived

    chain.start()

    def first(k, start, size):
        chain.arrive(k)
        here = full.at[x, pl.ds(start, size), y, c]
        for d in offsets(4):
            there = device((x + d) % NX, z, y, c) if k in X_FIRST_B else device(x, z, (y + d) % NY, c)
            send(here, here, send_1.at[k, d - 1], recv_1.at[k, d - 1], there)

    def second(k, start, size):
        for d in offsets(4):
            arrived(full.at[x, pl.ds(start, size), y, c], send_1.at[k, d - 1], recv_1.at[k, d - 1])
        if k in X_FIRST_B:
            here = full.at[:, pl.ds(start, size), y, c]
        else:
            here = full.at[x, pl.ds(start, size), :, c]
        for d in offsets(4):
            there = device(x, z, (y + d) % NY, c) if k in X_FIRST_B else device((x + d) % NX, z, y, c)
            send(here, here, send_2.at[k, d - 1], recv_2.at[k, d - 1], there)

    def third(k, start, size):
        for d in offsets(4):
            arrived(full.at[:, pl.ds(start, size), y, c], send_2.at[k, d - 1], recv_2.at[k, d - 1])
        here = full.at[:, pl.ds(start, size), :, c]
        send(here, here, send_s.at[k], recv_s.at[k], sibling)

    grams = [jnp.zeros((R, R), F32)]

    def gram(block):
        return lax.dot_general(
            block, block, (((0,), (0,)), ((), ())), preferred_element_type=F32
        )

    def fourth(k, start, size):
        arrived(full.at[:, pl.ds(start, size), :, 1 - c], send_s.at[k], recv_s.at[k])
        for i in range(NX):
            block = full[i, start:start + size].reshape(size * NY * NC * PIECE, R)
            grams[0] = grams[0] + gram(block)

    parts = groups()
    stages = (first, second, third, fourth)
    for stage, k in schedule(GAPS_B):
        stages[stage](k, *parts[k])
        if (stage, k) == (0, 0):
            for i, d in enumerate((1, NY - 1)):
                there = device(x, z, (y + d) % NY, c)
                send(own_c.at[c_half(i)], full_c.at[g, c_half(i)], send_c.at[i], recv_c.at[i], there)
            send(own_c, full_c.at[g], send_c.at[2], recv_c.at[2], sibling)
            gram_c = gram(own_c[...])
        if (stage, k) == (1, 2):
            for i in range(2):
                arrived(full_c.at[g_across, c_half(i)], send_c.at[i], recv_c.at[i])
            send(full_c.at[g_across], full_c.at[g_across], send_c.at[3], recv_c.at[3], sibling)
            gram_c = gram_c + gram(full_c[g_across])
    for i, other in ((2, g + 1 - 2 * c), (3, g_across + 1 - 2 * c)):
        arrived(full_c.at[other], send_c.at[i], recv_c.at[i])
        gram_c = gram_c + gram(full_c[other])
    system_ref[...] = grams[0] * gram_c
    mover.finish()


def split(a):
    high = a.astype(BF16)
    return high, (a - high.astype(F32)).astype(BF16)


def three_pass(a, b):
    a_high, a_low = a
    b_high, b_low = b
    return jnp.dot(
        jnp.concatenate([a_high, a_low, a_high], axis=1),
        jnp.concatenate([b_high, b_high, b_low], axis=0),
        preferred_element_type=F32,
    )


def exact_dot(a, b):
    return jnp.dot(a, b, precision=lax.Precision.HIGHEST, preferred_element_type=F32)


def invert(system, out_ref, work):
    sub = lax.broadcasted_iota(jnp.int32, (R, R), 0)
    lane = lax.broadcasted_iota(jnp.int32, (R, R), 1)
    eye = jnp.where(sub == lane, 1.0, 0.0).astype(F32)
    diagonal = system * eye
    across = lax.rsqrt(jnp.sum(diagonal, axis=0, keepdims=True))
    down = lax.rsqrt(jnp.sum(diagonal, axis=1, keepdims=True))
    scaled = system * across * down
    bound = jnp.max(jnp.sum(jnp.abs(scaled), axis=0, keepdims=True), axis=1, keepdims=True)
    start = 1.0 / bound
    rest = eye - scaled * start
    guess = (eye + rest) * start
    for _ in range(7):
        rest_parts = split(rest)
        rest = three_pass(rest_parts, rest_parts)
        guess = guess + three_pass(split(rest), split(guess))
    work[...] = guess

    def unfinished(state):
        count, error = state
        return jnp.logical_and(count < 24, jnp.logical_not(error <= 1e-3))

    def refine(state):
        count, _ = state
        guess = work[...]
        rest = eye - exact_dot(guess, scaled)
        work[...] = guess + exact_dot(rest, guess)
        error = jnp.max(jnp.sum(jnp.abs(rest), axis=0, keepdims=True))
        return count + 1, error

    _, error = lax.while_loop(unfinished, refine, (jnp.int32(0), jnp.float32(1.0)))

    @pl.when(jnp.logical_not(error <= 1e-3))
    def _():
        work[...] = scaled

        def pivot(k, carry):
            a = work[...]
            row = work[pl.ds(k, 1), :]
            column = jnp.sum(jnp.where(lane == k, a, 0.0), axis=1, keepdims=True)
            value = jnp.sum(jnp.where(lane[:1] == k, row, 0.0), axis=1, keepdims=True)
            row = row / value
            updated = jnp.where(lane == k, -column / value, a - column * row)
            updated = jnp.where(sub == k, jnp.where(lane == k, 1.0 / value, row), updated)
            work[...] = updated
            return carry

        lax.fori_loop(0, R, pivot, 0)

    out_ref[...] = work[...] * across * down


def inverse_kernel(
    counts_ref, row_ref, col_ref, depth_ref, full_ref, c_ref, system_ref,
    inverse_ref, rows_b_ref, rows_c_ref, keep_ref, work,
):
    z = place()[1]
    live = counts_ref[0, 0]
    for s in range(NB):
        col = col_ref[0, 0, s]
        pair = lax.div(col, YH)
        slot = slot_at(lax.rem(pair, NZ), z)
        rows = full_ref[lax.div(pair, NZ), slot, pl.ds(lax.rem(col, YH) * 2, 2)]
        rows_b_ref[s] = rows.reshape(EDGE, R).astype(F32)
        depth = pl.multiple_of(depth_ref[0, 0, s] * EDGE, EDGE)
        rows_c_ref[s] = c_ref[pl.ds(depth, EDGE), :]
        for i in range(2):
            keep = jnp.logical_and(s < live, row_ref[0, 0, s] == i)
            keep_ref[s, i] = jnp.full((8, R), jnp.where(keep, 1, 0), jnp.int32)
    invert(system_ref[...], inverse_ref, work)


def update_kernel(
    values_ref, rows_b_ref, rows_c_ref, keep_ref, inverse_ref,
    a_ref, full,
    partial, weights, parts,
    send_g, recv_g, send_z, recv_z, send_1, recv_1, send_2, recv_2,
):
    x, z, y, c = place()
    yh, yl = y // 2, y % 2
    g = yl * NC + c
    facing = device(x, z, (y + 2) % NY, c)

    def member(other):
        return device(x, z, yh * 2 + other // NC, other % NC)

    others = [member((g + d) % 4) for d in range(1, 4)]
    others += [device(x, (z + d + NZ) % NZ, y, c) for d in (1, 2, -1, -2)]
    others += [device((x + d) % NX, z, y, c) for d in range(1, NX)]
    others += [facing]
    announce(others)

    partial[...] = jnp.zeros_like(partial)
    weights[...] = jnp.zeros_like(weights)
    chunks = EDGE * EDGE // R

    def slot_step(s, carry):
        for q in range(4):
            weights[q, q * EDGE:(q + 1) * EDGE, :] = rows_c_ref[s]
        b_rows = rows_b_ref[s]
        cube = jnp.concatenate(
            [values_ref[0, 0, s, :, t * R:(t + 1) * R] for t in range(chunks)], axis=0
        )
        term = jnp.zeros((EDGE, R), F32)
        for q in range(4):
            product = jnp.dot(cube, weights[q], preferred_element_type=F32)
            for t in range(chunks):
                j = t * 4 + q
                term += product[t * EDGE:(t + 1) * EDGE, :] * b_rows[j:j + 1, :]
        for i in range(2):
            keep = keep_ref[s, i][:1, :] > 0
            partial[i * EDGE:(i + 1) * EDGE, :] += jnp.where(keep, term, 0.0)
        return carry

    lax.fori_loop(0, NB, slot_step, 0)

    await_greetings(others)
    mover = Mover(facing)
    chain = Chain(mover, lambda i, n: full.at[x, pl.ds(i, n), yh], send_z, recv_z, x, z, y, c)
    send, arrived = mover.send, mover.arrived

    def own(other):
        return pl.ds(pl.multiple_of(other * ROWS, ROWS), ROWS)

    for d in (2, 1, 3):
        other = (g + d) % 4
        send(partial.at[own(other)], parts.at[d - 1], send_g.at[d - 1], recv_g.at[d - 1], member(other))
    total = partial[own(g), :]
    for d in (1, 3, 2):
        arrived(parts.at[d - 1], send_g.at[d - 1], recv_g.at[d - 1])
        total = total + parts[d - 1]
    solved = exact_dot(total, inverse_ref[...]).astype(BF16)
    a_ref[...] = solved
    full[x, 0, yh] = solved

    chain.start()

    def first(k, start, size):
        chain.arrive(k)
        here = full.at[x, pl.ds(start, size), yh]
        if k in X_FIRST_A:
            for d in offsets(NX):
                send(here, here, send_1.at[k, d - 1], recv_1.at[k, d - 1], device((x + d) % NX, z, y, c))
        else:
            send(here, here, send_1.at[k, 0], recv_1.at[k, 0], facing)

    def second(k, start, size):
        here = full.at[x, pl.ds(start, size), yh]
        if k in X_FIRST_A:
            for d in offsets(NX):
                arrived(here, send_1.at[k, d - 1], recv_1.at[k, d - 1])
            column = full.at[:, pl.ds(start, size), yh]
            send(column, column, send_2.at[k, 0], recv_2.at[k, 0], facing)
        else:
            arrived(here, send_1.at[k, 0], recv_1.at[k, 0])
            both = full.at[x, pl.ds(start, size)]
            for d in offsets(NX):
                send(both, both, send_2.at[k, d - 1], recv_2.at[k, d - 1], device((x + d) % NX, z, y, c))

    def third(k, start, size):
        if k in X_FIRST_A:
            arrived(full.at[:, pl.ds(start, size), yh], send_2.at[k, 0], recv_2.at[k, 0])
        else:
            for d in offsets(NX):
                arrived(full.at[x, pl.ds(start, size)], send_2.at[k, d - 1], recv_2.at[k, d - 1])

    order = groups()
    stages = (first, second, third)
    for stage, k in schedule(GAPS_A):
        stages[stage](k, *order[k])
    mover.finish()


def pick_kernel(fetch_ref, solved_ref, full, a_ref, fetched_ref, units):
    a_ref[...] = solved_ref[...]
    z = place()[1]

    def pick(s, carry):
        f = fetch_ref[0, 0, s]
        owner, within = lax.div(f, 2), lax.rem(f, 2)
        start = pl.multiple_of(within * PIECE, PIECE)
        pair = lax.div(owner, YH)
        slot = slot_at(lax.rem(pair, NZ), z)
        unit = full[lax.div(pair, NZ), slot, lax.rem(owner, YH), pl.ds(start, PIECE), :]
        unit = unit.astype(F32)
        for h in range(2):
            units[h, pl.ds(pl.multiple_of(s * PIECE, PIECE), PIECE), :] = unit[:, h * 128:(h + 1) * 128]
        return carry

    lax.fori_loop(0, SLOTS, pick, 0, unroll=16)
    for r in range(PIECE):
        for h in range(2):
            at = r * R + h * 128
            picked = units.at[h][pl.ds(r, SLOTS, stride=PIECE), :]
            fetched_ref[0, 0, :, at:at + 128] = picked.astype(BF16)


def dma(*shape):
    return pltpu.SemaphoreType.DMA(shape)


VMEM = pl.BlockSpec(memory_space=pltpu.VMEM)
SMEM = pl.BlockSpec(memory_space=pltpu.SMEM)
HBM = pl.BlockSpec(memory_space=pltpu.HBM)


def on_device(values, counts, row_block, col_block, depth_block, factor_b, factor_c, fetch_list):
    n_groups = len(groups())
    full_b, own_c, system = pl.pallas_call(
        gather_kernel,
        out_shape=(
            jax.ShapeDtypeStruct((NX, NZ, NY, NC, PIECE, R), BF16),
            jax.ShapeDtypeStruct((R, R), BF16),
            jax.ShapeDtypeStruct((R, R), F32),
        ),
        in_specs=[HBM] * 2,
        out_specs=(VMEM,) * 3,
        scratch_shapes=[
            pltpu.VMEM((4, R, R), BF16),
            dma(2), dma(n_groups + 1), dma(n_groups + 1), dma(n_groups, 3), dma(n_groups, 3),
            dma(n_groups, 3), dma(n_groups, 3), dma(n_groups), dma(n_groups), dma(4), dma(4),
        ],
        compiler_params=pltpu.CompilerParams(
            collective_id=0, has_side_effects=True, vmem_limit_bytes=24 << 20
        ),
        name="gather_factors",
    )(factor_b, factor_c)
    inverse, rows_b, rows_c, keep = pl.pallas_call(
        inverse_kernel,
        out_shape=(
            jax.ShapeDtypeStruct((R, R), F32),
            jax.ShapeDtypeStruct((NB, EDGE, R), F32),
            jax.ShapeDtypeStruct((NB, EDGE, R), BF16),
            jax.ShapeDtypeStruct((NB, 2, 8, R), jnp.int32),
        ),
        in_specs=[SMEM] * 4 + [VMEM] * 3,
        out_specs=(VMEM,) * 4,
        scratch_shapes=[pltpu.VMEM((R, R), F32)],
        compiler_params=pltpu.CompilerParams(vmem_limit_bytes=24 << 20),
        name="invert_select",
    )(counts, row_block, col_block, depth_block, full_b, own_c, system)
    solved, full_a = pl.pallas_call(
        update_kernel,
        out_shape=(
            jax.ShapeDtypeStruct((ROWS, R), BF16),
            jax.ShapeDtypeStruct((NX, NZ, YH, ROWS, R), BF16),
        ),
        in_specs=[VMEM] * 5,
        out_specs=(VMEM, VMEM),
        scratch_shapes=[
            pltpu.VMEM((2 * EDGE, R), F32),
            pltpu.VMEM((4, R, R), BF16),
            pltpu.VMEM((3, ROWS, R), F32),
            dma(3), dma(3), dma(n_groups + 1), dma(n_groups + 1), dma(n_groups, 3), dma(n_groups, 3),
            dma(n_groups, 3), dma(n_groups, 3),
        ],
        compiler_params=pltpu.CompilerParams(
            collective_id=1, has_side_effects=True, vmem_limit_bytes=24 << 20
        ),
        name="update_gather",
    )(values, rows_b, rows_c, keep, inverse)
    return pl.pallas_call(
        pick_kernel,
        out_shape=(
            jax.ShapeDtypeStruct((ROWS, R), BF16),
            jax.ShapeDtypeStruct((1, 1, SLOTS, PIECE * R), BF16),
        ),
        in_specs=[SMEM, VMEM, VMEM],
        out_specs=(VMEM, VMEM),
        scratch_shapes=[pltpu.VMEM((2, SLOTS * PIECE, 128), F32)],
        compiler_params=pltpu.CompilerParams(vmem_limit_bytes=16 << 20),
        name="pick_units",
    )(fetch_list, solved, full_a)


def solution(mesh):
    placed = (
        P("blk", "grp", None, None, None),
        P("blk", "grp"),
        P("blk", "grp", None),
        P("blk", "grp", None),
        P("blk", "grp", None),
        P("blk", None),
        P("grp", None),
        P("blk", "grp", None),
    )
    return jax.shard_map(
        on_device,
        mesh=mesh,
        in_specs=placed,
        out_specs=(P(("blk", "grp"), None), P("blk", "grp", None, None)),
        check_vma=False,
    )
```

```python
import functools

import jax
import jax.numpy as jnp
from jax import lax
from jax.experimental import pallas as pl
from jax.experimental.pallas import tpu as pltpu
from jax.sharding import PartitionSpec as P

MESH = pl.DeviceIdType.MESH
NX, NZ, NY, NC = 4, 16, 4, 2
YH = 2
R = 256
EDGE = 64
NB = 6
PIECE = 16
ROWS = 32
SLOTS = 64
F32 = jnp.float32
BF16 = jnp.bfloat16


def place():
    b, g = lax.axis_index("blk"), lax.axis_index("grp")
    x, z, yh = b // (NZ * YH), (b // YH) % NZ, b % YH
    return x, z, yh * 2 + g // NC, g % NC


def device(x, z, y, c):
    return ((x * NZ + z) * YH + y // 2, (y % 2) * NC + c)


def announce(others):
    barrier = pltpu.get_barrier_semaphore()
    for other in others:
        pl.semaphore_signal(barrier, inc=1, device_id=other, device_id_type=MESH)


def await_greetings(others):
    pl.semaphore_wait(pltpu.get_barrier_semaphore(), len(others))


def slot_at(z_there, z_here):
    d = lax.rem(z_here - z_there + NZ, NZ)
    left = d <= NZ // 2
    step = jnp.where(left, d, NZ - d) - 1
    slot = 4 * (step // 2) + step % 2 + jnp.where(left, 1, 3)
    return jnp.where(d == 0, 0, slot)


def groups():
    return [(0, 1)] + [(i, 2) for i in range(1, NZ - 1, 2)] + [(NZ - 1, 1)]


def offsets(n):
    order = []
    for d in range(1, n // 2 + 1):
        order.append(d)
        if n - d != d:
            order.append(n - d)
    return order


def schedule(gaps):
    events = []
    for k in range(len(groups())):
        time = (k + 1) // 2 * 2.2
        for stage in range(len(gaps) + 1):
            events.append((time + sum(gaps[:stage]), stage, k))
    return [event[1:] for event in sorted(events)]


class Mover:
    def __init__(self, other):
        self.sent, self.other = [], other

    def send(self, source, target, send_sem, recv_sem, device_id):
        copy = pltpu.make_async_remote_copy(
            src_ref=source, dst_ref=target, send_sem=send_sem, recv_sem=recv_sem,
            device_id=device_id, device_id_type=MESH,
        )
        copy.start()
        self.sent.append(copy)

    def arrived(self, target, send_sem, recv_sem):
        pltpu.make_async_remote_copy(
            src_ref=target, dst_ref=target, send_sem=send_sem, recv_sem=recv_sem,
            device_id=self.other, device_id_type=MESH,
        ).wait_recv()

    def finish(self):
        for copy in self.sent:
            copy.wait_send()


class Chain:
    def __init__(self, mover, at, send_sem, recv_sem, x, z, y, c):
        self.mover, self.at, self.send_sem, self.recv_sem = mover, at, send_sem, recv_sem
        self.place = x, z, y, c

    def peer(self, d):
        x, z, y, c = self.place
        return device(x, (z + d + NZ) % NZ, y, c)

    def start(self):
        for i, d in enumerate((1, 2, -1, -2)):
            self.mover.send(
                self.at(0, 1), self.at(1 + i, 1), self.send_sem.at[i], self.recv_sem.at[i], self.peer(d)
            )

    def arrive(self, k):
        order = groups()
        if k in (1, 2):
            for i in (2 * k - 2, 2 * k - 1):
                self.mover.arrived(self.at(1 + i, 1), self.send_sem.at[i], self.recv_sem.at[i])
        elif k > 2:
            self.mover.arrived(self.at(*order[k]), self.send_sem.at[k + 1], self.recv_sem.at[k + 1])
        if 1 <= k < len(order) - 2:
            start, size = order[k + 2]
            self.mover.send(
                self.at(order[k][0], size), self.at(start, size),
                self.send_sem.at[k + 3], self.recv_sem.at[k + 3], self.peer(2 if k % 2 else -2),
            )


GAPS_B = (2.3, 4.5, 2.2)
GAPS_A = (2.3, 4.5)
X_FIRST_B = (0, 2, 4, 6, 8)
X_FIRST_A = (0, 2, 3, 5, 6, 8)


def gather_kernel(
    b_ref, c_ref,
    full, own_c, system_ref,
    full_c,
    local_sem, send_z, recv_z, send_1, recv_1, send_2, recv_2, send_s, recv_s, send_c, recv_c,
):
    x, z, y, c = place()
    g = (y % 2) * NC + c
    sibling = device(x, z, y, 1 - c)
    g_across = g + 2 - 4 * (y % 2)

    def c_half(i):
        return pl.ds(i * R // 2, R // 2)

    own_rows = pl.ds(pl.multiple_of(g * PIECE, PIECE), PIECE)
    loads = [
        pltpu.make_async_copy(b_ref.at[own_rows], full.at[x, 0, y, c], local_sem.at[0]),
        pltpu.make_async_copy(c_ref, own_c, local_sem.at[1]),
    ]
    for load in loads:
        load.start()

    others = [device(x, (z + d + NZ) % NZ, y, c) for d in (1, 2, -1, -2)]
    others += [device((x + d) % NX, z, y, c) for d in range(1, NX)]
    others += [device(x, z, (y + d) % NY, c) for d in range(1, NY)]
    others += [sibling]
    announce(others)
    loads[0].wait()
    loads[1].wait()
    await_greetings(others)
    mover = Mover(sibling)
    chain = Chain(mover, lambda i, n: full.at[x, pl.ds(i, n), y, c], send_z, recv_z, x, z, y, c)
    send, arrived = mover.send, mover.arrived

    chain.start()

    def first(k, start, size):
        chain.arrive(k)
        here = full.at[x, pl.ds(start, size), y, c]
        for d in offsets(4):
            there = device((x + d) % NX, z, y, c) if k in X_FIRST_B else device(x, z, (y + d) % NY, c)
            send(here, here, send_1.at[k, d - 1], recv_1.at[k, d - 1], there)

    def second(k, start, size):
        for d in offsets(4):
            arrived(full.at[x, pl.ds(start, size), y, c], send_1.at[k, d - 1], recv_1.at[k, d - 1])
        if k in X_FIRST_B:
            here = full.at[:, pl.ds(start, size), y, c]
        else:
            here = full.at[x, pl.ds(start, size), :, c]
        for d in offsets(4):
            there = device(x, z, (y + d) % NY, c) if k in X_FIRST_B else device((x + d) % NX, z, y, c)
            send(here, here, send_2.at[k, d - 1], recv_2.at[k, d - 1], there)

    def third(k, start, size):
        for d in offsets(4):
            arrived(full.at[:, pl.ds(start, size), y, c], send_2.at[k, d - 1], recv_2.at[k, d - 1])
        here = full.at[:, pl.ds(start, size), :, c]
        send(here, here, send_s.at[k], recv_s.at[k], sibling)

    grams = [jnp.zeros((R, R), F32)]

    def gram(block):
        return lax.dot_general(
            block, block, (((0,), (0,)), ((), ())), preferred_element_type=F32
        )

    def fourth(k, start, size):
        arrived(full.at[:, pl.ds(start, size), :, 1 - c], send_s.at[k], recv_s.at[k])
        for i in range(NX):
            block = full[i, start:start + size].reshape(size * NY * NC * PIECE, R)
            grams[0] = grams[0] + gram(block)

    parts = groups()
    stages = (first, second, third, fourth)
    for stage, k in schedule(GAPS_B):
        stages[stage](k, *parts[k])
        if (stage, k) == (0, 0):
            for i, d in enumerate((1, NY - 1)):
                there = device(x, z, (y + d) % NY, c)
                send(own_c.at[c_half(i)], full_c.at[g, c_half(i)], send_c.at[i], recv_c.at[i], there)
            send(own_c, full_c.at[g], send_c.at[2], recv_c.at[2], sibling)
            gram_c = gram(own_c[...])
        if (stage, k) == (1, 2):
            for i in range(2):
                arrived(full_c.at[g_across, c_half(i)], send_c.at[i], recv_c.at[i])
            send(full_c.at[g_across], full_c.at[g_across], send_c.at[3], recv_c.at[3], sibling)
            gram_c = gram_c + gram(full_c[g_across])
    for i, other in ((2, g + 1 - 2 * c), (3, g_across + 1 - 2 * c)):
        arrived(full_c.at[other], send_c.at[i], recv_c.at[i])
        gram_c = gram_c + gram(full_c[other])
    system_ref[...] = grams[0] * gram_c
    mover.finish()


def split(a):
    high = a.astype(BF16)
    return high, (a - high.astype(F32)).astype(BF16)


def three_pass(a, b):
    a_high, a_low = a
    b_high, b_low = b
    return jnp.dot(
        jnp.concatenate([a_high, a_low, a_high], axis=1),
        jnp.concatenate([b_high, b_high, b_low], axis=0),
        preferred_element_type=F32,
    )


def exact_dot(a, b):
    return jnp.dot(a, b, precision=lax.Precision.HIGHEST, preferred_element_type=F32)


def invert(system, out_ref, work):
    sub = lax.broadcasted_iota(jnp.int32, (R, R), 0)
    lane = lax.broadcasted_iota(jnp.int32, (R, R), 1)
    eye = jnp.where(sub == lane, 1.0, 0.0).astype(F32)
    diagonal = system * eye
    across = lax.rsqrt(jnp.sum(diagonal, axis=0, keepdims=True))
    down = lax.rsqrt(jnp.sum(diagonal, axis=1, keepdims=True))
    scaled = system * across * down
    bound = jnp.max(jnp.sum(jnp.abs(scaled), axis=0, keepdims=True), axis=1, keepdims=True)
    start = 1.0 / bound
    rest = eye - scaled * start
    guess = (eye + rest) * start
    for _ in range(7):
        rest_parts = split(rest)
        rest = three_pass(rest_parts, rest_parts)
        guess = guess + three_pass(split(rest), split(guess))
    work[...] = guess

    def unfinished(state):
        count, error = state
        return jnp.logical_and(count < 24, jnp.logical_not(error <= 1e-3))

    def refine(state):
        count, _ = state
        guess = work[...]
        rest = eye - exact_dot(guess, scaled)
        work[...] = guess + exact_dot(rest, guess)
        error = jnp.max(jnp.sum(jnp.abs(rest), axis=0, keepdims=True))
        return count + 1, error

    _, error = lax.while_loop(unfinished, refine, (jnp.int32(0), jnp.float32(1.0)))

    @pl.when(jnp.logical_not(error <= 1e-3))
    def _():
        work[...] = scaled

        def pivot(k, carry):
            a = work[...]
            row = work[pl.ds(k, 1), :]
            column = jnp.sum(jnp.where(lane == k, a, 0.0), axis=1, keepdims=True)
            value = jnp.sum(jnp.where(lane[:1] == k, row, 0.0), axis=1, keepdims=True)
            row = row / value
            updated = jnp.where(lane == k, -column / value, a - column * row)
            updated = jnp.where(sub == k, jnp.where(lane == k, 1.0 / value, row), updated)
            work[...] = updated
            return carry

        lax.fori_loop(0, R, pivot, 0)

    out_ref[...] = work[...] * across * down


def inverse_kernel(
    counts_ref, row_hbm, col_hbm, depth_hbm, full_ref, c_ref, system_ref,
    inverse_ref, rows_b_ref, rows_c_ref, keep_ref, work, row_ref, col_ref, depth_ref, load_sem,
):
    loads = [
        pltpu.make_async_copy(source, target, load_sem.at[i])
        for i, (source, target) in enumerate(
            ((row_hbm, row_ref), (col_hbm, col_ref), (depth_hbm, depth_ref))
        )
    ]
    for load in loads:
        load.start()
    invert(system_ref[...], inverse_ref, work)
    for load in loads:
        load.wait()
    z = place()[1]
    live = counts_ref[0, 0]
    for s in range(NB):
        col = col_ref[0, 0, s]
        pair = lax.div(col, YH)
        slot = slot_at(lax.rem(pair, NZ), z)
        rows = full_ref[lax.div(pair, NZ), slot, pl.ds(lax.rem(col, YH) * 2, 2)]
        rows_b_ref[s] = rows.reshape(EDGE, R).astype(F32)
        depth = pl.multiple_of(depth_ref[0, 0, s] * EDGE, EDGE)
        rows_c_ref[s] = c_ref[pl.ds(depth, EDGE), :]
        for i in range(2):
            keep = jnp.logical_and(s < live, row_ref[0, 0, s] == i)
            keep_ref[s, i] = jnp.full((8, R), jnp.where(keep, 1, 0), jnp.int32)


def update_kernel(
    values_ref, rows_b_ref, rows_c_ref, keep_ref, inverse_ref,
    a_ref, full,
    partial, weights, parts,
    send_g, recv_g, send_z, recv_z, send_1, recv_1, send_2, recv_2,
):
    x, z, y, c = place()
    yh, yl = y // 2, y % 2
    g = yl * NC + c
    facing = device(x, z, (y + 2) % NY, c)

    def member(other):
        return device(x, z, yh * 2 + other // NC, other % NC)

    others = [member((g + d) % 4) for d in range(1, 4)]
    others += [device(x, (z + d + NZ) % NZ, y, c) for d in (1, 2, -1, -2)]
    others += [device((x + d) % NX, z, y, c) for d in range(1, NX)]
    others += [facing]
    announce(others)

    partial[...] = jnp.zeros_like(partial)
    weights[...] = jnp.zeros_like(weights)
    chunks = EDGE * EDGE // R

    def slot_step(s, carry):
        for q in range(4):
            weights[q, q * EDGE:(q + 1) * EDGE, :] = rows_c_ref[s]
        b_rows = rows_b_ref[s]
        cube = jnp.concatenate(
            [values_ref[0, 0, s, :, t * R:(t + 1) * R] for t in range(chunks)], axis=0
        )
        term = jnp.zeros((EDGE, R), F32)
        for q in range(4):
            product = jnp.dot(cube, weights[q], preferred_element_type=F32)
            for t in range(chunks):
                j = t * 4 + q
                term += product[t * EDGE:(t + 1) * EDGE, :] * b_rows[j:j + 1, :]
        for i in range(2):
            keep = keep_ref[s, i][:1, :] > 0
            partial[i * EDGE:(i + 1) * EDGE, :] += jnp.where(keep, term, 0.0)
        return carry

    lax.fori_loop(0, NB, slot_step, 0)

    await_greetings(others)
    mover = Mover(facing)
    chain = Chain(mover, lambda i, n: full.at[x, pl.ds(i, n), yh], send_z, recv_z, x, z, y, c)
    send, arrived = mover.send, mover.arrived

    def own(other):
        return pl.ds(pl.multiple_of(other * ROWS, ROWS), ROWS)

    for d in (2, 1, 3):
        other = (g + d) % 4
        send(partial.at[own(other)], parts.at[d - 1], send_g.at[d - 1], recv_g.at[d - 1], member(other))
    total = partial[own(g), :]
    for d in (1, 3, 2):
        arrived(parts.at[d - 1], send_g.at[d - 1], recv_g.at[d - 1])
        total = total + parts[d - 1]
    solved = exact_dot(total, inverse_ref[...]).astype(BF16)
    a_ref[...] = solved
    full[x, 0, yh] = solved

    chain.start()

    def first(k, start, size):
        chain.arrive(k)
        here = full.at[x, pl.ds(start, size), yh]
        if k in X_FIRST_A:
            for d in offsets(NX):
                send(here, here, send_1.at[k, d - 1], recv_1.at[k, d - 1], device((x + d) % NX, z, y, c))
        else:
            send(here, here, send_1.at[k, 0], recv_1.at[k, 0], facing)

    def second(k, start, size):
        here = full.at[x, pl.ds(start, size), yh]
        if k in X_FIRST_A:
            for d in offsets(NX):
                arrived(here, send_1.at[k, d - 1], recv_1.at[k, d - 1])
            column = full.at[:, pl.ds(start, size), yh]
            send(column, column, send_2.at[k, 0], recv_2.at[k, 0], facing)
        else:
            arrived(here, send_1.at[k, 0], recv_1.at[k, 0])
            both = full.at[x, pl.ds(start, size)]
            for d in offsets(NX):
                send(both, both, send_2.at[k, d - 1], recv_2.at[k, d - 1], device((x + d) % NX, z, y, c))

    def third(k, start, size):
        if k in X_FIRST_A:
            arrived(full.at[:, pl.ds(start, size), yh], send_2.at[k, 0], recv_2.at[k, 0])
        else:
            for d in offsets(NX):
                arrived(full.at[x, pl.ds(start, size)], send_2.at[k, d - 1], recv_2.at[k, d - 1])

    order = groups()
    stages = (first, second, third)
    for stage, k in schedule(GAPS_A):
        stages[stage](k, *order[k])
    mover.finish()


def pick_kernel(fetch_ref, solved_ref, full, a_ref, fetched_ref, units):
    a_ref[...] = solved_ref[...]
    z = place()[1]

    def pick(s, carry):
        f = fetch_ref[0, 0, s]
        owner, within = lax.div(f, 2), lax.rem(f, 2)
        start = pl.multiple_of(within * PIECE, PIECE)
        pair = lax.div(owner, YH)
        slot = slot_at(lax.rem(pair, NZ), z)
        unit = full[lax.div(pair, NZ), slot, lax.rem(owner, YH), pl.ds(start, PIECE), :]
        unit = unit.astype(F32)
        for h in range(2):
            units[h, pl.ds(pl.multiple_of(s * PIECE, PIECE), PIECE), :] = unit[:, h * 128:(h + 1) * 128]
        return carry

    lax.fori_loop(0, SLOTS, pick, 0, unroll=16)
    for r in range(PIECE):
        for h in range(2):
            at = r * R + h * 128
            picked = units.at[h][pl.ds(r, SLOTS, stride=PIECE), :]
            fetched_ref[0, 0, :, at:at + 128] = picked.astype(BF16)


def dma(*shape):
    return pltpu.SemaphoreType.DMA(shape)


VMEM = pl.BlockSpec(memory_space=pltpu.VMEM)
SMEM = pl.BlockSpec(memory_space=pltpu.SMEM)
HBM = pl.BlockSpec(memory_space=pltpu.HBM)


def in_hbm(x):
    return pltpu.with_memory_space_constraint(x, pltpu.HBM)


def on_device(values, counts, row_block, col_block, depth_block, factor_b, factor_c, fetch_list):
    n_groups = len(groups())
    full_b, own_c, system = pl.pallas_call(
        gather_kernel,
        out_shape=(
            jax.ShapeDtypeStruct((NX, NZ, NY, NC, PIECE, R), BF16),
            jax.ShapeDtypeStruct((R, R), BF16),
            jax.ShapeDtypeStruct((R, R), F32),
        ),
        in_specs=[HBM] * 2,
        out_specs=(VMEM,) * 3,
        scratch_shapes=[
            pltpu.VMEM((4, R, R), BF16),
            dma(2), dma(n_groups + 1), dma(n_groups + 1), dma(n_groups, 3), dma(n_groups, 3),
            dma(n_groups, 3), dma(n_groups, 3), dma(n_groups), dma(n_groups), dma(4), dma(4),
        ],
        compiler_params=pltpu.CompilerParams(
            collective_id=0, has_side_effects=True, vmem_limit_bytes=24 << 20
        ),
        name="gather_factors",
    )(in_hbm(factor_b), in_hbm(factor_c))
    inverse, rows_b, rows_c, keep = pl.pallas_call(
        inverse_kernel,
        out_shape=(
            jax.ShapeDtypeStruct((R, R), F32),
            jax.ShapeDtypeStruct((NB, EDGE, R), F32),
            jax.ShapeDtypeStruct((NB, EDGE, R), BF16),
            jax.ShapeDtypeStruct((NB, 2, 8, R), jnp.int32),
        ),
        in_specs=[SMEM] + [HBM] * 3 + [VMEM] * 3,
        out_specs=(VMEM,) * 4,
        scratch_shapes=[pltpu.VMEM((R, R), F32)] + [pltpu.SMEM((1, 1, NB), jnp.int32)] * 3 + [dma(3)],
        compiler_params=pltpu.CompilerParams(vmem_limit_bytes=24 << 20),
        name="invert_select",
    )(counts, in_hbm(row_block), in_hbm(col_block), in_hbm(depth_block), full_b, own_c, system)
    solved, full_a = pl.pallas_call(
        update_kernel,
        out_shape=(
            jax.ShapeDtypeStruct((ROWS, R), BF16),
            jax.ShapeDtypeStruct((NX, NZ, YH, ROWS, R), BF16),
        ),
        in_specs=[VMEM] * 5,
        out_specs=(VMEM, VMEM),
        scratch_shapes=[
            pltpu.VMEM((2 * EDGE, R), F32),
            pltpu.VMEM((4, R, R), BF16),
            pltpu.VMEM((3, ROWS, R), F32),
            dma(3), dma(3), dma(n_groups + 1), dma(n_groups + 1), dma(n_groups, 3), dma(n_groups, 3),
            dma(n_groups, 3), dma(n_groups, 3),
        ],
        compiler_params=pltpu.CompilerParams(
            collective_id=1, has_side_effects=True, vmem_limit_bytes=24 << 20
        ),
        name="update_gather",
    )(values, rows_b, rows_c, keep, inverse)
    return pl.pallas_call(
        pick_kernel,
        out_shape=(
            jax.ShapeDtypeStruct((ROWS, R), BF16),
            jax.ShapeDtypeStruct((1, 1, SLOTS, PIECE * R), BF16),
        ),
        in_specs=[SMEM, VMEM, VMEM],
        out_specs=(VMEM, VMEM),
        scratch_shapes=[pltpu.VMEM((2, SLOTS * PIECE, 128), F32)],
        compiler_params=pltpu.CompilerParams(vmem_limit_bytes=16 << 20),
        name="pick_units",
    )(fetch_list, solved, full_a)


def solution(mesh):
    placed = (
        P("blk", "grp", None, None, None),
        P("blk", "grp"),
        P("blk", "grp", None),
        P("blk", "grp", None),
        P("blk", "grp", None),
        P("blk", None),
        P("grp", None),
        P("blk", "grp", None),
    )
    return jax.shard_map(
        on_device,
        mesh=mesh,
        in_specs=placed,
        out_specs=(P(("blk", "grp"), None), P("blk", "grp", None, None)),
        check_vma=False,
    )
```

```python
import functools

import jax
import jax.numpy as jnp
from jax import lax
from jax.experimental import pallas as pl
from jax.experimental.pallas import tpu as pltpu
from jax.sharding import PartitionSpec as P

MESH = pl.DeviceIdType.MESH
NX, NZ, NY, NC = 4, 16, 4, 2
YH = 2
R = 256
EDGE = 64
NB = 6
PIECE = 16
ROWS = 32
SLOTS = 64
F32 = jnp.float32
BF16 = jnp.bfloat16


def place():
    b, g = lax.axis_index("blk"), lax.axis_index("grp")
    x, z, yh = b // (NZ * YH), (b // YH) % NZ, b % YH
    return x, z, yh * 2 + g // NC, g % NC


def device(x, z, y, c):
    return ((x * NZ + z) * YH + y // 2, (y % 2) * NC + c)


def announce(others):
    barrier = pltpu.get_barrier_semaphore()
    for other in others:
        pl.semaphore_signal(barrier, inc=1, device_id=other, device_id_type=MESH)


def await_greetings(others):
    pl.semaphore_wait(pltpu.get_barrier_semaphore(), len(others))


def slot_at(z_there, z_here):
    d = lax.rem(z_here - z_there + NZ, NZ)
    left = d <= NZ // 2
    step = jnp.where(left, d, NZ - d) - 1
    slot = 4 * (step // 2) + step % 2 + jnp.where(left, 1, 3)
    return jnp.where(d == 0, 0, slot)


def groups():
    return [(0, 1)] + [(i, 2) for i in range(1, NZ - 1, 2)] + [(NZ - 1, 1)]


def offsets(n):
    order = []
    for d in range(1, n // 2 + 1):
        order.append(d)
        if n - d != d:
            order.append(n - d)
    return order


def schedule(gaps):
    events = []
    for k in range(len(groups())):
        time = (k + 1) // 2 * 2.2
        for stage in range(len(gaps) + 1):
            events.append((time + sum(gaps[:stage]), stage, k))
    return [event[1:] for event in sorted(events)]


class Mover:
    def __init__(self, other):
        self.sent, self.other = [], other

    def send(self, source, target, send_sem, recv_sem, device_id):
        copy = pltpu.make_async_remote_copy(
            src_ref=source, dst_ref=target, send_sem=send_sem, recv_sem=recv_sem,
            device_id=device_id, device_id_type=MESH,
        )
        copy.start()
        self.sent.append(copy)

    def arrived(self, target, send_sem, recv_sem):
        pltpu.make_async_remote_copy(
            src_ref=target, dst_ref=target, send_sem=send_sem, recv_sem=recv_sem,
            device_id=self.other, device_id_type=MESH,
        ).wait_recv()

    def finish(self):
        for copy in self.sent:
            copy.wait_send()


class Chain:
    def __init__(self, mover, at, send_sem, recv_sem, x, z, y, c):
        self.mover, self.at, self.send_sem, self.recv_sem = mover, at, send_sem, recv_sem
        self.place = x, z, y, c

    def peer(self, d):
        x, z, y, c = self.place
        return device(x, (z + d + NZ) % NZ, y, c)

    def start(self):
        for i, d in enumerate((1, 2, -1, -2)):
            self.mover.send(
                self.at(0, 1), self.at(1 + i, 1), self.send_sem.at[i], self.recv_sem.at[i], self.peer(d)
            )

    def arrive(self, k):
        order = groups()
        if k in (1, 2):
            for i in (2 * k - 2, 2 * k - 1):
                self.mover.arrived(self.at(1 + i, 1), self.send_sem.at[i], self.recv_sem.at[i])
        elif k > 2:
            self.mover.arrived(self.at(*order[k]), self.send_sem.at[k + 1], self.recv_sem.at[k + 1])
        if 1 <= k < len(order) - 2:
            start, size = order[k + 2]
            self.mover.send(
                self.at(order[k][0], size), self.at(start, size),
                self.send_sem.at[k + 3], self.recv_sem.at[k + 3], self.peer(2 if k % 2 else -2),
            )


GAPS_B = (2.3, 4.5, 2.2)
GAPS_A = (2.3, 4.5)
X_FIRST_B = (0, 2, 4, 6, 8)
X_FIRST_A = (0, 2, 3, 5, 6, 8)


def gather_kernel(
    b_ref, c_ref,
    full, own_c, system_ref,
    full_c,
    local_sem, send_z, recv_z, send_1, recv_1, send_2, recv_2, send_s, recv_s, send_c, recv_c,
):
    x, z, y, c = place()
    g = (y % 2) * NC + c
    sibling = device(x, z, y, 1 - c)
    g_across = g + 2 - 4 * (y % 2)

    def c_half(i):
        return pl.ds(i * R // 2, R // 2)

    own_rows = pl.ds(pl.multiple_of(g * PIECE, PIECE), PIECE)
    loads = [
        pltpu.make_async_copy(b_ref.at[own_rows], full.at[x, 0, y, c], local_sem.at[0]),
        pltpu.make_async_copy(c_ref, own_c, local_sem.at[1]),
    ]
    for load in loads:
        load.start()

    others = [device(x, (z + d + NZ) % NZ, y, c) for d in (1, 2, -1, -2)]
    others += [device((x + d) % NX, z, y, c) for d in range(1, NX)]
    others += [device(x, z, (y + d) % NY, c) for d in range(1, NY)]
    others += [sibling]
    announce(others)
    loads[0].wait()
    loads[1].wait()
    await_greetings(others)
    mover = Mover(sibling)
    chain = Chain(mover, lambda i, n: full.at[x, pl.ds(i, n), y, c], send_z, recv_z, x, z, y, c)
    send, arrived = mover.send, mover.arrived

    chain.start()

    def first(k, start, size):
        chain.arrive(k)
        here = full.at[x, pl.ds(start, size), y, c]
        for d in offsets(4):
            there = device((x + d) % NX, z, y, c) if k in X_FIRST_B else device(x, z, (y + d) % NY, c)
            send(here, here, send_1.at[k, d - 1], recv_1.at[k, d - 1], there)

    def second(k, start, size):
        for d in offsets(4):
            arrived(full.at[x, pl.ds(start, size), y, c], send_1.at[k, d - 1], recv_1.at[k, d - 1])
        if k in X_FIRST_B:
            here = full.at[:, pl.ds(start, size), y, c]
        else:
            here = full.at[x, pl.ds(start, size), :, c]
        for d in offsets(4):
            there = device(x, z, (y + d) % NY, c) if k in X_FIRST_B else device((x + d) % NX, z, y, c)
            send(here, here, send_2.at[k, d - 1], recv_2.at[k, d - 1], there)

    def third(k, start, size):
        for d in offsets(4):
            arrived(full.at[:, pl.ds(start, size), y, c], send_2.at[k, d - 1], recv_2.at[k, d - 1])
        here = full.at[:, pl.ds(start, size), :, c]
        send(here, here, send_s.at[k], recv_s.at[k], sibling)

    grams = [jnp.zeros((R, R), F32)]

    def gram(block):
        return lax.dot_general(
            block, block, (((0,), (0,)), ((), ())), preferred_element_type=F32
        )

    def fourth(k, start, size):
        arrived(full.at[:, pl.ds(start, size), :, 1 - c], send_s.at[k], recv_s.at[k])
        for i in range(NX):
            block = full[i, start:start + size].reshape(size * NY * NC * PIECE, R)
            grams[0] = grams[0] + gram(block)

    parts = groups()
    stages = (first, second, third, fourth)
    for stage, k in schedule(GAPS_B):
        stages[stage](k, *parts[k])
        if (stage, k) == (0, 0):
            for i, d in enumerate((1, NY - 1)):
                there = device(x, z, (y + d) % NY, c)
                send(own_c.at[c_half(i)], full_c.at[g, c_half(i)], send_c.at[i], recv_c.at[i], there)
            send(own_c, full_c.at[g], send_c.at[2], recv_c.at[2], sibling)
            gram_c = gram(own_c[...])
        if (stage, k) == (1, 2):
            for i in range(2):
                arrived(full_c.at[g_across, c_half(i)], send_c.at[i], recv_c.at[i])
            send(full_c.at[g_across], full_c.at[g_across], send_c.at[3], recv_c.at[3], sibling)
            gram_c = gram_c + gram(full_c[g_across])
    for i, other in ((2, g + 1 - 2 * c), (3, g_across + 1 - 2 * c)):
        arrived(full_c.at[other], send_c.at[i], recv_c.at[i])
        gram_c = gram_c + gram(full_c[other])
    system_ref[...] = grams[0] * gram_c
    mover.finish()


def split(a):
    high = a.astype(BF16)
    return high, (a - high.astype(F32)).astype(BF16)


def three_pass(a, b):
    a_high, a_low = a
    b_high, b_low = b
    return jnp.dot(
        jnp.concatenate([a_high, a_low, a_high], axis=1),
        jnp.concatenate([b_high, b_high, b_low], axis=0),
        preferred_element_type=F32,
    )


def exact_dot(a, b):
    return jnp.dot(a, b, precision=lax.Precision.HIGHEST, preferred_element_type=F32)


def invert(system, out_ref, work):
    sub = lax.broadcasted_iota(jnp.int32, (R, R), 0)
    lane = lax.broadcasted_iota(jnp.int32, (R, R), 1)
    eye = jnp.where(sub == lane, 1.0, 0.0).astype(F32)
    diagonal = system * eye
    across = lax.rsqrt(jnp.sum(diagonal, axis=0, keepdims=True))
    down = lax.rsqrt(jnp.sum(diagonal, axis=1, keepdims=True))
    scaled = system * across * down
    bound = jnp.max(jnp.sum(jnp.abs(scaled), axis=0, keepdims=True), axis=1, keepdims=True)
    start = 1.0 / bound
    rest = eye - scaled * start
    guess = (eye + rest) * start
    rest_parts = split(rest)
    rest = three_pass(rest_parts, rest_parts)
    for _ in range(6):
        both = three_pass(split(rest), split(jnp.concatenate([rest, guess], axis=1)))
        rest, guess = both[:, :R], guess + both[:, R:]
    guess = guess + three_pass(split(rest), split(guess))
    work[...] = guess

    def unfinished(state):
        count, error = state
        return jnp.logical_and(count < 24, jnp.logical_not(error <= 1e-3))

    def refine(state):
        count, _ = state
        guess = work[...]
        rest = eye - exact_dot(guess, scaled)
        work[...] = guess + exact_dot(rest, guess)
        error = jnp.max(jnp.sum(jnp.abs(rest), axis=0, keepdims=True))
        return count + 1, error

    _, error = lax.while_loop(unfinished, refine, (jnp.int32(0), jnp.float32(1.0)))

    @pl.when(jnp.logical_not(error <= 1e-3))
    def _():
        work[...] = scaled

        def pivot(k, carry):
            a = work[...]
            row = work[pl.ds(k, 1), :]
            column = jnp.sum(jnp.where(lane == k, a, 0.0), axis=1, keepdims=True)
            value = jnp.sum(jnp.where(lane[:1] == k, row, 0.0), axis=1, keepdims=True)
            row = row / value
            updated = jnp.where(lane == k, -column / value, a - column * row)
            updated = jnp.where(sub == k, jnp.where(lane == k, 1.0 / value, row), updated)
            work[...] = updated
            return carry

        lax.fori_loop(0, R, pivot, 0)

    out_ref[...] = work[...] * across * down


def inverse_kernel(
    counts_ref, row_hbm, col_hbm, depth_hbm, full_ref, c_ref, system_ref,
    inverse_ref, rows_b_ref, rows_c_ref, keep_ref, work, row_ref, col_ref, depth_ref, load_sem,
):
    loads = [
        pltpu.make_async_copy(source, target, load_sem.at[i])
        for i, (source, target) in enumerate(
            ((row_hbm, row_ref), (col_hbm, col_ref), (depth_hbm, depth_ref))
        )
    ]
    for load in loads:
        load.start()
    invert(system_ref[...], inverse_ref, work)
    for load in loads:
        load.wait()
    z = place()[1]
    live = counts_ref[0, 0]
    for s in range(NB):
        col = col_ref[0, 0, s]
        pair = lax.div(col, YH)
        slot = slot_at(lax.rem(pair, NZ), z)
        rows = full_ref[lax.div(pair, NZ), slot, pl.ds(lax.rem(col, YH) * 2, 2)]
        rows_b_ref[s] = rows.reshape(EDGE, R).astype(F32)
        depth = pl.multiple_of(depth_ref[0, 0, s] * EDGE, EDGE)
        rows_c_ref[s] = c_ref[pl.ds(depth, EDGE), :]
        for i in range(2):
            keep = jnp.logical_and(s < live, row_ref[0, 0, s] == i)
            keep_ref[s, i] = jnp.full((8, R), jnp.where(keep, 1, 0), jnp.int32)


def update_kernel(
    values_ref, rows_b_ref, rows_c_ref, keep_ref, inverse_ref,
    a_ref, full,
    partial, weights, parts,
    send_g, recv_g, send_z, recv_z, send_1, recv_1, send_2, recv_2,
):
    x, z, y, c = place()
    yh, yl = y // 2, y % 2
    g = yl * NC + c
    facing = device(x, z, (y + 2) % NY, c)

    def member(other):
        return device(x, z, yh * 2 + other // NC, other % NC)

    others = [member((g + d) % 4) for d in range(1, 4)]
    others += [device(x, (z + d + NZ) % NZ, y, c) for d in (1, 2, -1, -2)]
    others += [device((x + d) % NX, z, y, c) for d in range(1, NX)]
    others += [facing]
    announce(others)

    partial[...] = jnp.zeros_like(partial)
    weights[...] = jnp.zeros_like(weights)
    chunks = EDGE * EDGE // R

    def slot_step(s, carry):
        for q in range(4):
            weights[q, q * EDGE:(q + 1) * EDGE, :] = rows_c_ref[s]
        b_rows = rows_b_ref[s]
        cube = jnp.concatenate(
            [values_ref[0, 0, s, :, t * R:(t + 1) * R] for t in range(chunks)], axis=0
        )
        term = jnp.zeros((EDGE, R), F32)
        for q in range(4):
            product = jnp.dot(cube, weights[q], preferred_element_type=F32)
            for t in range(chunks):
                j = t * 4 + q
                term += product[t * EDGE:(t + 1) * EDGE, :] * b_rows[j:j + 1, :]
        for i in range(2):
            keep = keep_ref[s, i][:1, :] > 0
            partial[i * EDGE:(i + 1) * EDGE, :] += jnp.where(keep, term, 0.0)
        return carry

    lax.fori_loop(0, NB, slot_step, 0)

    await_greetings(others)
    mover = Mover(facing)
    chain = Chain(mover, lambda i, n: full.at[x, pl.ds(i, n), yh], send_z, recv_z, x, z, y, c)
    send, arrived = mover.send, mover.arrived

    def own(other):
        return pl.ds(pl.multiple_of(other * ROWS, ROWS), ROWS)

    for d in (2, 1, 3):
        other = (g + d) % 4
        send(partial.at[own(other)], parts.at[d - 1], send_g.at[d - 1], recv_g.at[d - 1], member(other))
    total = partial[own(g), :]
    for d in (1, 3, 2):
        arrived(parts.at[d - 1], send_g.at[d - 1], recv_g.at[d - 1])
        total = total + parts[d - 1]
    solved = exact_dot(total, inverse_ref[...]).astype(BF16)
    a_ref[...] = solved
    full[x, 0, yh] = solved

    chain.start()

    def first(k, start, size):
        chain.arrive(k)
        here = full.at[x, pl.ds(start, size), yh]
        if k in X_FIRST_A:
            for d in offsets(NX):
                send(here, here, send_1.at[k, d - 1], recv_1.at[k, d - 1], device((x + d) % NX, z, y, c))
        else:
            send(here, here, send_1.at[k, 0], recv_1.at[k, 0], facing)

    def second(k, start, size):
        here = full.at[x, pl.ds(start, size), yh]
        if k in X_FIRST_A:
            for d in offsets(NX):
                arrived(here, send_1.at[k, d - 1], recv_1.at[k, d - 1])
            column = full.at[:, pl.ds(start, size), yh]
            send(column, column, send_2.at[k, 0], recv_2.at[k, 0], facing)
        else:
            arrived(here, send_1.at[k, 0], recv_1.at[k, 0])
            both = full.at[x, pl.ds(start, size)]
            for d in offsets(NX):
                send(both, both, send_2.at[k, d - 1], recv_2.at[k, d - 1], device((x + d) % NX, z, y, c))

    def third(k, start, size):
        if k in X_FIRST_A:
            arrived(full.at[:, pl.ds(start, size), yh], send_2.at[k, 0], recv_2.at[k, 0])
        else:
            for d in offsets(NX):
                arrived(full.at[x, pl.ds(start, size)], send_2.at[k, d - 1], recv_2.at[k, d - 1])

    order = groups()
    stages = (first, second, third)
    for stage, k in schedule(GAPS_A):
        stages[stage](k, *order[k])
    mover.finish()


def pick_kernel(fetch_ref, solved_ref, full, a_ref, fetched_ref, units):
    a_ref[...] = solved_ref[...]
    z = place()[1]

    def pick(s, carry):
        f = fetch_ref[0, 0, s]
        owner, within = lax.div(f, 2), lax.rem(f, 2)
        start = pl.multiple_of(within * PIECE, PIECE)
        pair = lax.div(owner, YH)
        slot = slot_at(lax.rem(pair, NZ), z)
        unit = full[lax.div(pair, NZ), slot, lax.rem(owner, YH), pl.ds(start, PIECE), :]
        unit = unit.astype(F32)
        for h in range(2):
            units[h, pl.ds(pl.multiple_of(s * PIECE, PIECE), PIECE), :] = unit[:, h * 128:(h + 1) * 128]
        return carry

    lax.fori_loop(0, SLOTS, pick, 0, unroll=16)
    for r in range(PIECE):
        for h in range(2):
            at = r * R + h * 128
            picked = units.at[h][pl.ds(r, SLOTS, stride=PIECE), :]
            fetched_ref[0, 0, :, at:at + 128] = picked.astype(BF16)


def dma(*shape):
    return pltpu.SemaphoreType.DMA(shape)


VMEM = pl.BlockSpec(memory_space=pltpu.VMEM)
SMEM = pl.BlockSpec(memory_space=pltpu.SMEM)
HBM = pl.BlockSpec(memory_space=pltpu.HBM)


def in_hbm(x):
    return pltpu.with_memory_space_constraint(x, pltpu.HBM)


def on_device(values, counts, row_block, col_block, depth_block, factor_b, factor_c, fetch_list):
    n_groups = len(groups())
    full_b, own_c, system = pl.pallas_call(
        gather_kernel,
        out_shape=(
            jax.ShapeDtypeStruct((NX, NZ, NY, NC, PIECE, R), BF16),
            jax.ShapeDtypeStruct((R, R), BF16),
            jax.ShapeDtypeStruct((R, R), F32),
        ),
        in_specs=[HBM] * 2,
        out_specs=(VMEM,) * 3,
        scratch_shapes=[
            pltpu.VMEM((4, R, R), BF16),
            dma(2), dma(n_groups + 1), dma(n_groups + 1), dma(n_groups, 3), dma(n_groups, 3),
            dma(n_groups, 3), dma(n_groups, 3), dma(n_groups), dma(n_groups), dma(4), dma(4),
        ],
        compiler_params=pltpu.CompilerParams(
            collective_id=0, has_side_effects=True, vmem_limit_bytes=24 << 20
        ),
        name="gather_factors",
    )(in_hbm(factor_b), in_hbm(factor_c))
    inverse, rows_b, rows_c, keep = pl.pallas_call(
        inverse_kernel,
        out_shape=(
            jax.ShapeDtypeStruct((R, R), F32),
            jax.ShapeDtypeStruct((NB, EDGE, R), F32),
            jax.ShapeDtypeStruct((NB, EDGE, R), BF16),
            jax.ShapeDtypeStruct((NB, 2, 8, R), jnp.int32),
        ),
        in_specs=[SMEM] + [HBM] * 3 + [VMEM] * 3,
        out_specs=(VMEM,) * 4,
        scratch_shapes=[pltpu.VMEM((R, R), F32)] + [pltpu.SMEM((1, 1, NB), jnp.int32)] * 3 + [dma(3)],
        compiler_params=pltpu.CompilerParams(vmem_limit_bytes=24 << 20),
        name="invert_select",
    )(counts, in_hbm(row_block), in_hbm(col_block), in_hbm(depth_block), full_b, own_c, system)
    solved, full_a = pl.pallas_call(
        update_kernel,
        out_shape=(
            jax.ShapeDtypeStruct((ROWS, R), BF16),
            jax.ShapeDtypeStruct((NX, NZ, YH, ROWS, R), BF16),
        ),
        in_specs=[VMEM] * 5,
        out_specs=(VMEM, VMEM),
        scratch_shapes=[
            pltpu.VMEM((2 * EDGE, R), F32),
            pltpu.VMEM((4, R, R), BF16),
            pltpu.VMEM((3, ROWS, R), F32),
            dma(3), dma(3), dma(n_groups + 1), dma(n_groups + 1), dma(n_groups, 3), dma(n_groups, 3),
            dma(n_groups, 3), dma(n_groups, 3),
        ],
        compiler_params=pltpu.CompilerParams(
            collective_id=1, has_side_effects=True, vmem_limit_bytes=24 << 20
        ),
        name="update_gather",
    )(values, rows_b, rows_c, keep, inverse)
    return pl.pallas_call(
        pick_kernel,
        out_shape=(
            jax.ShapeDtypeStruct((ROWS, R), BF16),
            jax.ShapeDtypeStruct((1, 1, SLOTS, PIECE * R), BF16),
        ),
        in_specs=[SMEM, VMEM, VMEM],
        out_specs=(VMEM, VMEM),
        scratch_shapes=[pltpu.VMEM((2, SLOTS * PIECE, 128), F32)],
        compiler_params=pltpu.CompilerParams(vmem_limit_bytes=16 << 20),
        name="pick_units",
    )(fetch_list, solved, full_a)


def solution(mesh):
    placed = (
        P("blk", "grp", None, None, None),
        P("blk", "grp"),
        P("blk", "grp", None),
        P("blk", "grp", None),
        P("blk", "grp", None),
        P("blk", None),
        P("grp", None),
        P("blk", "grp", None),
    )
    return jax.shard_map(
        on_device,
        mesh=mesh,
        in_specs=placed,
        out_specs=(P(("blk", "grp"), None), P("blk", "grp", None, None)),
        check_vma=False,
    )
```
